128 devices in a mesh: dom: 8 (over y, core), sub: 16 (over x, z).
Axes of the slice: x: 4, y: 4, z: 4, core: 2. Of those that a mesh axis runs over, the one named last changes fastest.
Arguments:
- adjoint_traces: bfloat16 [144, 1048576], P(None, ('dom', 'sub')), may hold values from -6 to 6
- primal_traces: bfloat16 [144, 1048576], P(None, ('dom', 'sub')), may hold values from -6 to 6
- jacobian: float32 [1048576], P(('dom', 'sub')), may hold values from 0.4 to 2.5
- stiffness: float32 [1048576], P(('dom', 'sub')), as said below
- connect: int32 [4, 1048576], P(None, ('dom', 'sub')), may hold values from 0 to 2047
- shared_perm: int32 [8, 16, 256], P('dom', 'sub'), may hold values from 0 to 255, each once within a row
- wall_owner: int32 [262144, 1], P(('dom', 'sub')), may hold values from 0 to 127; in each aligned block of 2048 rows (0 to 2047, 2048 to 4095, ...) at most 40 rows name the same one
- wall_patch: int32 [262144], P(('dom', 'sub')), may hold values from 0 to 15
- w_trace: bfloat16 [144, 384], replicated, may hold values from -0.5 to 0.5
- w_state: bfloat16 [144, 384], replicated, may hold values from -0.5 to 0.5
- w_node: bfloat16 [384, 12], replicated, may hold values from -1.25 to 1.25
- w_block: bfloat16 [384, 128], replicated, may hold values from -0.3125 to 0.3125
- w_adjoint: bfloat16 [12, 128], replicated, may hold values from -1.75 to 1.75
- stiff_ref: float32 [12, 12], replicated, as said below
Outputs:
- patch_grad: float32 [2048, 128], P(('dom', 'sub'))
- node_adjoint: float32 [3, 262144], P(None, ('dom', 'sub'))
The draws below stay inside these ranges and needn't reach their ends.
Inputs may be any that keep to these rules, and one draw needn't show every extreme that they name: `shared_perm`: each partition's row is a permutation. `wall_owner`: among the 2048 wall elements of one partition no owner is named more than 40 times, a bound that some block reaches. `stiffness`: each entry lies between 0.15 and 6. `stiff_ref`: symmetric; each diagonal entry exceeds the sum of magnitudes of the other entries of its row.
All inputs are finite; a program needn't handle non-finite values.
Results may differ from the reference program's by a relative error of at most 0.0029.
Values sent between devices are 32-bit elements; how exact they have to be, the bound alone decides.
No kernel may reach another device: no remote copies, remote signals or barrier semaphores. Data moves between devices by JAX's collectives and lax.ppermute only.
A program may use at most 64 MiB of HBM per device.

```python
import math
import jax
import jax.numpy as jnp
import numpy as np
from jax import lax

TRACE = 144
QUAD = 384
PARAMS = 128
PATCH_DEV = 16
ELEMS = 8192
WALL = 2048
NODES = 2048
SHARED = 256
CAP = 40
N_DOM = 8
N_SUB = 16
DEVICES = 128


def draw_stiffness(key, part):
    key = jax.random.fold_in(key, 11)
    key_group, key_elem = jax.random.split(key)
    part_count = N_DOM * N_SUB
    factor = jnp.exp(jax.random.uniform(key_group, (part_count, 1), jnp.float32, math.log(0.15), math.log(1.5)))
    spread = jnp.exp(jax.random.uniform(key_elem, (part_count, ELEMS), jnp.float32, 0.0, math.log(4.0)))
    return (factor * spread).reshape(-1)


def draw_stiff_ref(key, part):
    key = jax.random.fold_in(key, 7)
    key_diag, key_pair, key_same, key_cross, key_sign = jax.random.split(key, 5)
    diag_lo, diag_hi, same_lo, same_hi, cross_lo, cross_hi = (1.0, 1.4, 0.16, 0.22, 0.04, 0.06)
    index = jnp.arange(12, dtype=jnp.int32)
    component = index // 4
    corner_id = index % 4
    low_index = jnp.minimum(index[:, None], index[None, :])
    high_index = jnp.maximum(index[:, None], index[None, :])
    same_mag = jax.random.uniform(key_same, (12, 12), jnp.float32, same_lo, same_hi)[low_index, high_index]
    cross_mag = jax.random.uniform(key_cross, (12, 12), jnp.float32, cross_lo, cross_hi)[low_index, high_index]
    cross_sign = (jax.random.randint(key_sign, (12, 12), 0, 2) * 2 - 1).astype(jnp.float32)[low_index, high_index]
    pair_raw = (jax.random.randint(key_pair, (3, 3), 0, 2) * 2 - 1).astype(jnp.float32)
    comp_low = jnp.minimum(component[:, None], component[None, :])
    comp_high = jnp.maximum(component[:, None], component[None, :])
    pair_sign = pair_raw[comp_low, comp_high]
    same_corner = corner_id[:, None] == corner_id[None, :]
    on_diag = index[:, None] == index[None, :]
    off_vals = jnp.where(same_corner, pair_sign * same_mag, cross_sign * cross_mag)
    off_vals = jnp.where(on_diag, 0.0, off_vals)
    diag_vals = jax.random.uniform(key_diag, (12,), jnp.float32, diag_lo, diag_hi)
    return off_vals + jnp.where(on_diag, diag_vals[:, None], 0.0)


def place_ends(array, key, smallest, high):
    spot = [jax.random.randint(jax.random.fold_in(key, axis), (), 0, length) for axis, length in enumerate(array.shape)]
    widest = array.shape.index(max(array.shape))
    next_to = spot[:widest] + [(spot[widest] + 1) % array.shape[widest]] + spot[widest + 1:]
    return array.at[tuple(spot)].set(smallest).at[tuple(next_to)].set(high)


def block_scale(key, extent, pieces, least, top_value):
    def one(position, shards_of):
        steps = jax.random.uniform(jax.random.fold_in(jax.random.fold_in(key, 6), position), (shards_of,), jnp.float32, least / len(pieces), top_value / len(pieces))
        return jnp.repeat(jnp.exp(steps), extent[position] // shards_of).reshape((-1,) + (1,) * (len(extent) - position - 1))

    loudness = one(*pieces[0])
    for cut in pieces[1:]:
        loudness = loudness * one(*cut)
    return loudness


def deal_out(rng, own, number, rows, amount, top, bound, lean):
    order = jax.random.permutation(rng, amount)
    packed, ordinary = load_shares(amount, rows * top, bound, lean, True), load_shares(amount, rows * top, bound, lean, False)
    places = jnp.arange(amount)

    def named(lengths, rotation):
        used = int((lengths > 0).sum())
        fixed = max(1, used // 4)
        shifted = fixed + (places - fixed + rotation * (used - fixed)) % max(1, amount - fixed)
        return jnp.zeros((amount,), jnp.int32).at[order[jnp.where(places < fixed, places, shifted)]].set(jnp.asarray(lengths, jnp.int32))

    lengths = jnp.where(number % 4 == 0, named(packed, number // 4), named(ordinary, number - number // 4 - 1))
    mixed = jax.random.permutation(jax.random.fold_in(own, 3), amount)
    giver, sink = mixed[0:amount // 2 * 2:2], mixed[1:amount // 2 * 2:2]
    slack = jnp.minimum(lengths[giver] - 1, bound - lengths[sink]) // 2
    slack = jnp.where((giver == order[0]) | (sink == order[0]) | (lengths[sink] == 0), 0, jnp.maximum(slack, 0))
    shifted = jax.random.randint(jax.random.fold_in(own, 4), (amount // 2,), 0, 1 << 20) % (slack + 1)
    lengths = lengths.at[giver].add(-shifted).at[sink].add(shifted)
    items = jnp.searchsorted(jnp.cumsum(lengths), jnp.arange(rows * top), side="right").astype(jnp.int32)
    table = items.reshape(top, rows).T
    table = table[jax.random.permutation(jax.random.fold_in(own, 1), rows)]
    rotation = jax.random.randint(jax.random.fold_in(own, 2), (rows, 1), 0, top)
    return jnp.take_along_axis(table, (jnp.arange(top)[None, :] + rotation) % top, axis=1)


def load_shares(amount, total, reach, lean, full):
    portions = [(1 << 20) // math.isqrt(grade ** lean) + 1 for grade in range(1, amount + 1)]
    largest = reach if full else min(reach, max(-(-total // amount), total * portions[0] // sum(portions)))
    least = 1 if total - largest >= amount - 1 else 0
    counts, rest = [largest] + [least] * (amount - 1), total - largest - least * (amount - 1)
    while rest > 0:
        movable = [i for i in range(1, amount) if counts[i] < largest] or [i for i in range(1, amount) if counts[i] < reach]
        whole, left = sum([portions[i] for i in movable]), rest
        for i in movable:
            addition = min(reach - counts[i], max(1, left * portions[i] // whole), rest)
            counts[i] = counts[i] + addition
            rest = rest - addition
    return np.array(counts)


def normal_values(stream_key, dims, width, limit, cuts=(), kind=jnp.bfloat16):
    drawn = width * jax.random.normal(stream_key, dims, jnp.float32)
    if cuts:
        drawn = drawn * block_scale(stream_key, dims, cuts, -0.22, 0.18)
    return jnp.clip(drawn, -limit, limit).astype(kind)


def setup_inputs(seed: int = 0) -> dict:
    keys = jax.random.split(jax.random.key(seed), 15)
    adjoint_traces = normal_values(keys[0], (TRACE, DEVICES * ELEMS), 1.0, 6.0, ((1, 128),))
    primal_traces = normal_values(keys[1], (TRACE, DEVICES * ELEMS), 1.0, 6.0, ((1, 128),))
    jacobian = jnp.clip(jnp.exp(math.log(2.5) - 1.8325814 * jax.random.uniform(keys[2], (DEVICES * ELEMS,), jnp.float32) ** block_scale(keys[2], (DEVICES * ELEMS,), ((0, 128),), -0.2, 0.2)), 0.4, 2.5)
    stiffness = draw_stiffness(jax.random.fold_in(keys[14], 71), 0)
    connect = place_ends(jax.random.randint(keys[4], (4, DEVICES * ELEMS), 0, NODES), jax.random.fold_in(keys[4], 1), 0, NODES - 1).astype(jnp.int32)
    shared_perm = jax.vmap(lambda own: jax.random.permutation(own, SHARED))(jax.random.split(keys[5], N_DOM * N_SUB)).reshape((N_DOM, N_SUB, SHARED)).astype(jnp.int32)
    wall_owner_keys = jax.random.split(jax.random.fold_in(keys[6], 1), (DEVICES * WALL) // WALL)
    wall_owner_turns = jax.random.permutation(jax.random.fold_in(keys[6], 3), (DEVICES * WALL) // WALL)
    wall_owner = jax.vmap(lambda own, number: deal_out(jax.random.fold_in(keys[6], 2), own, number, WALL, DEVICES, 1, CAP, 1))(wall_owner_keys, wall_owner_turns).reshape((DEVICES * WALL, 1))
    wall_patch = place_ends(jax.random.randint(keys[7], (DEVICES * WALL,), 0, PATCH_DEV), jax.random.fold_in(keys[7], 1), 0, PATCH_DEV - 1).astype(jnp.int32)
    w_trace = normal_values(keys[8], (TRACE, QUAD), TRACE ** -0.5, 0.5)
    w_state = normal_values(keys[9], (TRACE, QUAD), TRACE ** -0.5, 0.5)
    w_node = normal_values(keys[10], (QUAD, 12), (QUAD // 16) ** -0.5, 1.25)
    w_block = normal_values(keys[11], (QUAD, PARAMS), QUAD ** -0.5, 0.3125)
    w_adjoint = normal_values(keys[12], (12, PARAMS), 12 ** -0.5, 1.75)
    stiff_ref = draw_stiff_ref(jax.random.fold_in(keys[14], 71), 0)
    return dict(adjoint_traces=adjoint_traces, primal_traces=primal_traces, jacobian=jacobian, stiffness=stiffness, connect=connect, shared_perm=shared_perm, wall_owner=wall_owner, wall_patch=wall_patch, w_trace=w_trace, w_state=w_state, w_node=w_node, w_block=w_block, w_adjoint=w_adjoint, stiff_ref=stiff_ref)


mass_shift = 0.5
relax = 0.7


def element_front(traces, states, jac_part, w_trace, w_state, w_node):
    upsilon = jnp.dot(w_trace.T, traces, preferred_element_type=jnp.float32)
    tangent = jnp.dot(w_state.T, states, preferred_element_type=jnp.float32)
    product = (jac_part[None, :] * upsilon * tangent).astype(jnp.bfloat16)
    node_terms = jnp.dot(w_node.T, product, preferred_element_type=jnp.float32)
    return node_terms, product


def assemble(values, conn_part, node_count):
    flat_values = values.reshape(3, -1)
    return jnp.zeros((3, node_count), jnp.float32).at[:, conn_part.reshape(-1)].add(flat_values)


def at_elements(node_field, conn_part):
    return node_field[:, conn_part.reshape(-1)].reshape(12, -1)


def share_all(fields, shared_perm):
    node_count = fields.shape[-1]
    rim_width = shared_perm.shape[-1]
    upper_rim = fields[..., node_count - rim_width:]
    lower_rim = fields[..., :rim_width]
    perm_index = jnp.broadcast_to(shared_perm[:, :, None, :], lower_rim.shape)
    lower_perm = jnp.take_along_axis(lower_rim, perm_index, axis=3)
    summed = upper_rim[:, :-1] + lower_perm[:, 1:]
    new_upper = jnp.concatenate([summed, upper_rim[:, -1:]], axis=1)
    new_perm = jnp.concatenate([lower_perm[:, :1], summed], axis=1)
    inverse = jnp.broadcast_to(jnp.argsort(shared_perm, axis=-1)[:, :, None, :], lower_rim.shape).astype(jnp.int32)
    new_lower = jnp.take_along_axis(new_perm, inverse, axis=3)
    return jnp.concatenate([new_lower, fields[..., rim_width:node_count - rim_width], new_upper], axis=3)


def reference(adjoint_traces, primal_traces, jacobian, stiffness, connect, shared_perm, wall_owner, wall_patch, w_trace, w_state, w_node, w_block, w_adjoint, stiff_ref):
    devices = N_DOM * N_SUB
    ref_diag = jnp.diagonal(stiff_ref)

    def front(part_id):
        base = part_id * ELEMS
        conn_part = lax.dynamic_slice_in_dim(connect, base, ELEMS, 1)
        stiff_part = lax.dynamic_slice_in_dim(stiffness, base, ELEMS, 0)

        def one_block(block_id):
            start = base + block_id * WALL
            return element_front(lax.dynamic_slice_in_dim(adjoint_traces, start, WALL, 1),
                                 lax.dynamic_slice_in_dim(primal_traces, start, WALL, 1),
                                 lax.dynamic_slice_in_dim(jacobian, start, WALL, 0),
                                 w_trace, w_state, w_node)

        terms, products = lax.map(one_block, jnp.arange(ELEMS // WALL, dtype=jnp.int32))
        node_terms = jnp.moveaxis(terms, 0, 1).reshape(12, ELEMS)
        sens_part = assemble(node_terms, conn_part, NODES)
        diag_part = assemble(stiff_part[None, :] * ref_diag[:, None], conn_part, NODES)
        return jnp.concatenate([sens_part, diag_part], axis=0), products[0]

    fronts, wall_products = lax.map(front, jnp.arange(devices, dtype=jnp.int32))
    shared = share_all(fronts.reshape(N_DOM, N_SUB, 6, NODES), shared_perm).reshape(devices, 6, NODES)
    sens_sum = shared[:, :3]
    diagonal = mass_shift + shared[:, 3:]
    psi_one = relax * sens_sum / diagonal

    def apply_part(part_id):
        base = part_id * ELEMS
        conn_part = lax.dynamic_slice_in_dim(connect, base, ELEMS, 1)
        stiff_part = lax.dynamic_slice_in_dim(stiffness, base, ELEMS, 0)
        element_vals = at_elements(psi_one[part_id], conn_part)
        pushed = stiff_part[None, :] * jnp.dot(stiff_ref, element_vals, precision=lax.Precision.HIGHEST)
        return assemble(pushed, conn_part, NODES)

    applied = lax.map(apply_part, jnp.arange(devices, dtype=jnp.int32))
    applied = share_all(applied.reshape(N_DOM, N_SUB, 3, NODES), shared_perm).reshape(devices, 3, NODES)
    psi_two = psi_one + relax * (sens_sum - (mass_shift * psi_one + applied)) / diagonal

    def wall_part(part_id):
        conn_wall = lax.dynamic_slice_in_dim(connect, part_id * ELEMS, WALL, 1)
        psi_wall = at_elements(psi_two[part_id], conn_wall)
        first = jnp.dot(wall_products[part_id].T, w_block, preferred_element_type=jnp.float32)
        second = jnp.dot(psi_wall.T, w_adjoint.astype(jnp.float32), precision=lax.Precision.HIGHEST)
        return first + second

    blocks = lax.map(wall_part, jnp.arange(devices, dtype=jnp.int32)).reshape(devices * WALL, PARAMS)
    patch_ids = (wall_owner.reshape(-1) * PATCH_DEV + wall_patch).astype(jnp.int32)
    patch_grad = jax.ops.segment_sum(blocks, patch_ids, num_segments=devices * PATCH_DEV)
    node_adjoint = jnp.moveaxis(psi_two, 0, 1).reshape(3, devices * NODES)
    return (patch_grad, node_adjoint)
```

```python
import functools

import jax
import jax.numpy as jnp
from jax import lax
from jax.experimental import pallas as pl
from jax.experimental.pallas import tpu as pltpu
from jax.sharding import PartitionSpec as P

PATCH_DEV = 16
LANES = 128
HIS = 16
FIELDS = 3
RIM = 256

mass_shift = 0.5
relax = 0.7

f32 = jnp.float32
bf16 = jnp.bfloat16
VMEM_LIMIT = 60 * 2**20

NN = (((1,), (0,)), ((), ()))
NT = (((1,), (1,)), ((), ()))


def mxu(a, b, dims):
    return lax.dot_general(a, b, dims, preferred_element_type=f32)


def exact(a, b, dims):
    return lax.dot_general(
        a, b, dims, preferred_element_type=f32, precision=lax.Precision.HIGHEST
    )


def halves(x):
    top = x.astype(bf16).astype(f32)
    return top, x - top


def one_hot(index_row, rows):
    shape = (rows, index_row.shape[1])
    wanted = jnp.broadcast_to(index_row.astype(jnp.int16), shape)
    hit = wanted == lax.broadcasted_iota(jnp.int16, shape, 0)
    return jnp.where(hit, jnp.ones(shape, bf16), jnp.zeros(shape, bf16))


def placed(index_row, value_rows):
    shape = (HIS, index_row.shape[1])
    wanted = jnp.broadcast_to(index_row.astype(jnp.int16), shape)
    hit = wanted == lax.broadcasted_iota(jnp.int16, shape, 0)
    zero = jnp.zeros(shape, bf16)
    return jnp.concatenate(
        [jnp.where(hit, jnp.broadcast_to(v, shape).astype(bf16), zero) for v in value_rows], axis=0
    )


def rim_rows(field, first):
    count = field.shape[0] // HIS
    parts = [
        jnp.concatenate([field[f * HIS + first + k : f * HIS + first + k + 1] for f in range(count)], 0)
        for k in range(2)
    ]
    return jnp.concatenate(parts, axis=1)


def reorder(rows, perm_row, dims):
    count = rows.shape[0]
    table = one_hot(perm_row, RIM)
    first, rest = halves(rows)
    second, third = halves(rest)
    pad = jnp.zeros((-count % 8, RIM), f32)
    stack = jnp.concatenate([first, pad, second, pad, third, pad], axis=0).astype(bf16)
    out = mxu(stack, table, dims)
    step = count + (-count % 8)
    return out[:count] + out[step : step + count] + out[2 * step : 2 * step + count]


def add_rims(field, below, above, perm_row):
    count = field.shape[0] // HIS
    place = lax.axis_index("sub")
    last = lax.axis_size("sub") - 1
    below = jnp.where(place == 0, 0.0, below)
    above = jnp.where(place == last, 0.0, above)
    low = reorder(below, perm_row, NT)
    parts = []
    for f in range(count):
        rows = field[f * HIS : (f + 1) * HIS]
        extra = jnp.concatenate(
            [
                low[f : f + 1, :LANES],
                low[f : f + 1, LANES:],
                jnp.zeros((HIS - 4, LANES), f32),
                above[f : f + 1, :LANES],
                above[f : f + 1, LANES:],
            ],
            axis=0,
        )
        parts.append(rows + extra)
    return jnp.concatenate(parts, axis=0)


def front_kernel(
    traces, states, jac, stiff, conn, perm, ref, w_trace, w_state, w_node, w_block,
    field, up, low, blocks,
    trace_t, state_t, node_t, block_t, sens, weight,
):
    step = pl.program_id(0)

    @pl.when(step == 0)
    def _():
        trace_t[...] = w_trace[...].astype(f32).T.astype(bf16)
        state_t[...] = w_state[...].astype(f32).T.astype(bf16)
        padded = jnp.concatenate(
            [w_node[...].astype(f32).T, jnp.zeros((4, w_node.shape[0]), f32)], axis=0
        )
        node_t[...] = padded.astype(bf16)
        block_t[...] = w_block[...].astype(f32).T.astype(bf16)
        sens[...] = jnp.zeros(sens.shape, f32)
        weight[...] = jnp.zeros(weight.shape, f32)

    upsilon = mxu(trace_t[...], traces[...], NN)
    tangent = mxu(state_t[...], states[...], NN)
    product = (jac[...] * upsilon * tangent).astype(bf16)
    terms = mxu(node_t[...], product, NN)

    @pl.when(step == 0)
    def _():
        blocks[...] = mxu(block_t[...], product, NN)

    top, rest = halves(terms)
    stiff_top, stiff_rest = halves(stiff[...])
    slots = conn[...]
    high, lane = slots >> 7, slots & (LANES - 1)
    for a in range(4):
        rows = [top[c * 4 + a : c * 4 + a + 1] for c in range(FIELDS)] + [stiff_top]
        rows += [rest[c * 4 + a : c * 4 + a + 1] for c in range(FIELDS)] + [stiff_rest]
        spread = placed(high[a : a + 1], rows)
        out = mxu(spread, one_hot(lane[a : a + 1], LANES), NT)
        cut = FIELDS * HIS
        sens[...] += out[:cut] + out[cut + HIS : 2 * cut + HIS]
        weight[a * HIS : (a + 1) * HIS] += out[cut : cut + HIS] + out[2 * cut + HIS :]

    @pl.when(step == pl.num_programs(0) - 1)
    def _():
        diag = []
        for c in range(FIELDS):
            total = jnp.zeros((HIS, LANES), f32)
            for a in range(4):
                i = c * 4 + a
                total += ref[i : i + 1, i : i + 1] * weight[a * HIS : (a + 1) * HIS]
            diag.append(total)
        both = jnp.concatenate([sens[...]] + diag, axis=0)
        field[...] = both
        up[...] = rim_rows(both, HIS - 2)
        low[...] = reorder(rim_rows(both, 0), perm[...], NN)


def wall_kernel(blocks, owner, patch, sums):
    count = sums.shape[0]
    slot = patch[...] * (count // PATCH_DEV) + owner[...]
    table = one_hot(slot, count)
    top, rest = halves(blocks[...])
    both = jnp.concatenate([top, rest], axis=0).astype(bf16)
    out = mxu(table, both, NT)
    sums[...] = out[:, :LANES] + out[:, LANES:]


def looked_up(table, slots):
    count = table.shape[0] // HIS
    n = slots.shape[1] // LANES
    rows = [[] for _ in range(count)]
    for k in range(n):
        here = slots[:, k * LANES : (k + 1) * LANES]
        high, lane = here >> 7, here & (LANES - 1)
        for f in range(count):
            got = jnp.zeros((8, LANES), f32)
            for h in range(HIS):
                line = jnp.broadcast_to(table[f * HIS + h : f * HIS + h + 1], (8, LANES))
                picked = jnp.take_along_axis(line, lane, axis=1, mode="promise_in_bounds")
                got = jnp.where(high == h, picked, got)
            rows[f].append(got)
    return [jnp.concatenate(r, axis=1) for r in rows]


def apply_kernel(
    field, below, above, conn, stiff, perm, ref,
    base, scale, applied, up, low,
    *, chunk,
):
    shared = add_rims(field[...], below[...], above[...], perm[...])
    cut = FIELDS * HIS
    sens, diag = shared[:cut], shared[cut:] + mass_shift
    over = relax / diag
    psi = over * sens
    base[...] = psi + over * (sens - mass_shift * psi)
    scale[...] = over

    index = lax.broadcasted_iota(jnp.int32, (24, 12), 0)
    pick = (index // 8 * 4 + index % 4) == lax.broadcasted_iota(jnp.int32, (24, 12), 1)
    pick = pick.astype(f32)
    wide = exact(exact(pick, ref[...], NN), pick, NT)
    half_of_row = lax.broadcasted_iota(jnp.int32, (24, 24), 0) // 4 % 2
    half_of_col = lax.broadcasted_iota(jnp.int32, (24, 24), 1) // 4 % 2
    wide = jnp.where(half_of_row == half_of_col, wide, 0.0)
    wide_top, wide_rest = halves(wide)
    wide = jnp.concatenate(
        [
            jnp.concatenate([wide_top, wide_top], axis=1),
            jnp.concatenate([wide_rest, wide_rest], axis=1),
        ],
        axis=0,
    ).astype(bf16)

    half = conn.shape[1] // 2
    total = jnp.zeros((cut, LANES), f32)
    for start in range(0, half, chunk):
        first = slice(start, start + chunk)
        second = slice(half + start, half + start + chunk)
        slots = jnp.concatenate([conn[:, first], conn[:, second]], axis=0)
        values = jnp.concatenate(looked_up(psi, slots), axis=0)
        top, rest = halves(values)
        pushed = mxu(wide, jnp.concatenate([top, rest], axis=0).astype(bf16), NN)
        pushed = pushed[:24] + pushed[24:]
        in_first = lax.broadcasted_iota(jnp.int32, (8, chunk), 0) < 4
        weight = jnp.where(in_first, stiff[:, first], stiff[:, second])
        pushed = pushed * jnp.concatenate([weight] * FIELDS, axis=0)
        top, rest = halves(pushed)
        high, lane = slots >> 7, slots & (LANES - 1)
        for row in range(8):
            rows = [x[c * 8 + row : c * 8 + row + 1] for x in (top, rest) for c in range(FIELDS)]
            spread = placed(high[row : row + 1], rows)
            out = mxu(spread, one_hot(lane[row : row + 1], LANES), NT)
            total += out[:cut] + out[cut:]
    applied[...] = total
    up[...] = rim_rows(total, HIS - 2)
    low[...] = reorder(rim_rows(total, 0), perm[...], NN)


def patch_kernel(
    base, scale, applied, below, above, conn, owner, patch, perm, w_adjoint, sums,
    adjoint, payload,
):
    psi = base[...] - scale[...] * add_rims(applied[...], below[...], above[...], perm[...])
    for c in range(FIELDS):
        for h in range(HIS):
            adjoint[c : c + 1, h * LANES : (h + 1) * LANES] = psi[c * HIS + h : c * HIS + h + 1]
    half = conn.shape[1] // 2
    slots = jnp.concatenate([conn[:, :half], conn[:, half:]], axis=0)
    values = looked_up(psi, slots)
    parts = [halves(v) for v in values]
    owners = payload.shape[0] // PATCH_DEV
    total = jnp.zeros((owners, 24 * PATCH_DEV), f32)
    for k in range(2):
        cols = slice(k * half, (k + 1) * half)
        rows = [
            parts[c][p][4 * k + a : 4 * k + a + 1]
            for p in range(2)
            for c in range(FIELDS)
            for a in range(4)
        ]
        spread = placed(patch[:, cols], rows)
        total += mxu(one_hot(owner[:, cols], owners), spread, NT)
    total = total[:, : 12 * PATCH_DEV] + total[:, 12 * PATCH_DEV :]
    top, rest = halves(total)
    both = jnp.concatenate([top, rest], axis=0).astype(bf16)
    patch_row = lax.broadcasted_iota(jnp.int32, (PATCH_DEV, LANES), 0)
    weights = w_adjoint[...].astype(f32)
    for q in range(PATCH_DEV):
        chosen = jnp.concatenate(
            [jnp.where(patch_row == q, weights[r : r + 1], 0.0) for r in range(12)], axis=0
        ).astype(bf16)
        out = mxu(both, chosen, NN)
        payload[pl.ds(q, owners, stride=PATCH_DEV), :] = (
            out[:owners] + out[owners:] + sums[q * owners : (q + 1) * owners]
        )


def params(flops, bytes_accessed):
    return dict(
        compiler_params=pltpu.CompilerParams(vmem_limit_bytes=VMEM_LIMIT),
        cost_estimate=pl.CostEstimate(
            flops=flops, bytes_accessed=bytes_accessed, transcendentals=0
        ),
    )


def exchanged(up, low):
    count = lax.axis_size("sub")
    below = lax.ppermute(up, "sub", [(i, (i + 1) % count) for i in range(count)])
    above = lax.ppermute(low, "sub", [(i, (i - 1) % count) for i in range(count)])
    return below, above


def per_device(
    adjoint_traces,
    primal_traces,
    jacobian,
    stiffness,
    connect,
    shared_perm,
    wall_owner,
    wall_patch,
    w_trace,
    w_state,
    w_node,
    w_block,
    w_adjoint,
    stiff_ref,
):
    elements = adjoint_traces.shape[1]
    walls = wall_owner.shape[0]
    devices = lax.axis_size("dom") * lax.axis_size("sub")
    width = w_block.shape[1]
    jac = jacobian.reshape(1, -1)
    stiff = stiffness.reshape(1, -1)
    owner = wall_owner.reshape(1, -1)
    patch = wall_patch.reshape(1, -1)
    perm = shared_perm.reshape(1, -1)
    cut = FIELDS * HIS

    def whole(shape):
        return pl.BlockSpec(shape, lambda s: (0,) * len(shape))

    def columns(rows):
        return pl.BlockSpec((rows, walls), lambda s: (0, s))

    def shape(*dims):
        return jax.ShapeDtypeStruct(dims, f32)

    trace, quad = w_trace.shape
    outs = [shape(2 * cut, LANES), shape(6, RIM), shape(6, RIM), shape(width, walls)]
    field, up, low, blocks = pl.pallas_call(
        front_kernel,
        grid=(elements // walls,),
        in_specs=[
            columns(trace), columns(trace), columns(1), columns(1), columns(4),
            whole(perm.shape), whole(stiff_ref.shape), whole(w_trace.shape),
            whole(w_state.shape), whole(w_node.shape), whole(w_block.shape),
        ],
        out_specs=[whole(o.shape) for o in outs],
        out_shape=outs,
        scratch_shapes=[
            pltpu.VMEM((quad, trace), bf16),
            pltpu.VMEM((quad, trace), bf16),
            pltpu.VMEM((16, quad), bf16),
            pltpu.VMEM((width, quad), bf16),
            pltpu.VMEM((cut, LANES), f32),
            pltpu.VMEM((4 * HIS, LANES), f32),
        ],
        name="front",
        **params(4 * elements * trace * quad, 4 * elements * trace),
    )(
        adjoint_traces, primal_traces, jac, stiff, connect, perm, stiff_ref,
        w_trace, w_state, w_node, w_block,
    )
    below, above = exchanged(up, low)

    sums = pl.pallas_call(
        wall_kernel,
        out_shape=shape(devices * PATCH_DEV, width),
        name="walls",
        **params(4 * walls * width * devices * PATCH_DEV, 8 * walls * width),
    )(blocks, owner, patch)

    small = shape(cut, LANES)
    base, scale, applied, up, low = pl.pallas_call(
        functools.partial(apply_kernel, chunk=512),
        out_shape=[small, small, small, shape(3, RIM), shape(3, RIM)],
        name="apply",
        **params(16 * elements * LANES * cut, 24 * elements),
    )(field, below, above, connect, stiff, perm, stiff_ref)
    below, above = exchanged(up, low)

    adjoint, payload = pl.pallas_call(
        patch_kernel,
        grid=(1,),
        in_specs=[
            whole(small.shape), whole(small.shape), whole(small.shape),
            whole(below.shape), whole(above.shape),
            pl.BlockSpec((4, walls), lambda s: (0, 0)),
            whole(owner.shape), whole(patch.shape), whole(perm.shape),
            whole(w_adjoint.shape), whole(sums.shape),
        ],
        out_specs=[whole((FIELDS, HIS * LANES)), whole(sums.shape)],
        out_shape=[shape(FIELDS, HIS * LANES), shape(*sums.shape)],
        name="patches",
        **params(64 * walls * LANES * cut, 8 * devices * PATCH_DEV * width),
    )(base, scale, applied, below, above, connect, owner, patch, perm, w_adjoint, sums)

    got = lax.all_to_all(
        payload.reshape(devices, PATCH_DEV, width),
        ("dom", "sub"),
        split_axis=0,
        concat_axis=0,
        tiled=True,
    )
    return (jnp.sum(got, axis=0), adjoint)


def solution(mesh):
    both = ("dom", "sub")
    return jax.shard_map(
        per_device,
        mesh=mesh,
        in_specs=(
            P(None, both),
            P(None, both),
            P(both),
            P(both),
            P(None, both),
            P("dom", "sub", None),
            P(both, None),
            P(both),
            P(),
            P(),
            P(),
            P(),
            P(),
            P(),
        ),
        out_specs=(P(both, None), P(None, both)),
        check_vma=False,
    )
```

```python
import functools

import jax
import jax.numpy as jnp
from jax import lax
from jax.experimental import pallas as pl
from jax.experimental.pallas import tpu as pltpu
from jax.sharding import PartitionSpec as P

PATCH_DEV = 16
LANES = 128
HIS = 16
FIELDS = 3
RIM = 256
GROUP = 4
KEPT = PATCH_DEV // GROUP
FRONT_VMEM = 40
ROWS = 8

mass_shift = 0.5
relax = 0.7

f32 = jnp.float32
bf16 = jnp.bfloat16

NN = (((1,), (0,)), ((), ()))
NT = (((1,), (1,)), ((), ()))


def mxu(a, b, dims):
    return lax.dot_general(a, b, dims, preferred_element_type=f32)


def exact(a, b, dims):
    return lax.dot_general(
        a, b, dims, preferred_element_type=f32, precision=lax.Precision.HIGHEST
    )


def halves(x):
    top = x.astype(bf16).astype(f32)
    return top, x - top


def one_hot(index_row, rows):
    shape = (rows, index_row.shape[1])
    wanted = jnp.broadcast_to(index_row.astype(jnp.int16), shape)
    hit = wanted == lax.broadcasted_iota(jnp.int16, shape, 0)
    return jnp.where(hit, jnp.ones(shape, bf16), jnp.zeros(shape, bf16))


def placed(index_row, value_rows):
    shape = (HIS, index_row.shape[1])
    wanted = jnp.broadcast_to(index_row.astype(jnp.int16), shape)
    hit = wanted == lax.broadcasted_iota(jnp.int16, shape, 0)
    zero = jnp.zeros(shape, bf16)
    return jnp.concatenate(
        [jnp.where(hit, jnp.broadcast_to(v, shape).astype(bf16), zero) for v in value_rows], axis=0
    )


def rim_rows(field, first):
    count = field.shape[0] // HIS
    parts = [
        jnp.concatenate([field[f * HIS + first + k : f * HIS + first + k + 1] for f in range(count)], 0)
        for k in range(2)
    ]
    return jnp.concatenate(parts, axis=1)


def reorder(rows, perm_row, dims):
    count = rows.shape[0]
    table = one_hot(perm_row, RIM)
    first, rest = halves(rows)
    second, third = halves(rest)
    pad = jnp.zeros((-count % 8, RIM), f32)
    stack = jnp.concatenate([first, pad, second, pad, third, pad], axis=0).astype(bf16)
    out = mxu(stack, table, dims)
    step = count + (-count % 8)
    return out[:count] + out[step : step + count] + out[2 * step : 2 * step + count]


def rims(below, above, perm_row):
    count = below.shape[0]
    place = lax.axis_index("sub")
    last = lax.axis_size("sub") - 1
    below = jnp.where(place == 0, 0.0, below)
    above = jnp.where(place == last, 0.0, above)
    low = reorder(below, perm_row, NT)
    parts = []
    for f in range(count):
        parts += [
            low[f : f + 1, :LANES],
            low[f : f + 1, LANES:],
            jnp.zeros((HIS - 4, LANES), f32),
            above[f : f + 1, :LANES],
            above[f : f + 1, LANES:],
        ]
    return jnp.concatenate(parts, axis=0)


def front_kernel(*refs, walls):
    sources, (field, up, low, blocks), held, sems = refs[:11], refs[11:15], refs[15:26], refs[26]
    traces, states, jac, stiff, conn, w_trace, w_state, w_node, w_block, perm, ref = held
    spans = [slice(s, s + walls) for s in range(0, traces.shape[1], walls)]
    copies = []

    def fetch(k, span=None):
        source, target = sources[k], held[k]
        if span is not None:
            source, target = source.at[:, span], target.at[:, span]
        copy = pltpu.make_async_copy(source, target, sems.at[len(copies)])
        copy.start()
        copies.append(copy)
        return copy

    weights = [fetch(k) for k in (5, 6, 7, 8)]
    first = [fetch(0, spans[0]), fetch(1, spans[0]), fetch(2)]
    small = [fetch(k) for k in (3, 4)]
    later = [[fetch(0, span), fetch(1, span)] for span in spans[1:]]
    last = [fetch(k) for k in (9, 10)]
    for copy in weights:
        copy.wait()
    trace_t = w_trace[...].astype(f32).T.astype(bf16)
    state_t = w_state[...].astype(f32).T.astype(bf16)
    pad = jnp.zeros((4, w_node.shape[1]), f32)
    node_t = jnp.concatenate([w_node[...].astype(f32), pad], axis=0).astype(bf16)
    block_t = w_block[...].astype(f32).T.astype(bf16)
    cut = FIELDS * HIS
    sens = jnp.zeros((cut, LANES), f32)
    weight = [jnp.zeros((HIS, LANES), f32) for _ in range(4)]
    for s, span in enumerate(spans):
        for copy in first if s == 0 else later[s - 1]:
            copy.wait()
        upsilon = mxu(trace_t, traces[:, span], NN)
        tangent = mxu(state_t, states[:, span], NN)
        product = (jac[:, span] * upsilon * tangent).astype(bf16)
        terms = mxu(node_t, product, NN)
        if s == 0:
            blocks[...] = mxu(block_t, product, NN)
            for copy in small:
                copy.wait()
        top, rest = halves(terms)
        stiff_top, stiff_rest = halves(stiff[:, span])
        slots = conn[:, span]
        high, lane = slots >> 7, slots & (LANES - 1)
        for a in range(4):
            rows = [top[c * 4 + a : c * 4 + a + 1] for c in range(FIELDS)] + [stiff_top]
            rows += [rest[c * 4 + a : c * 4 + a + 1] for c in range(FIELDS)] + [stiff_rest]
            spread = placed(high[a : a + 1], rows)
            out = mxu(spread, one_hot(lane[a : a + 1], LANES), NT)
            sens += out[:cut] + out[cut + HIS : 2 * cut + HIS]
            weight[a] += out[cut : cut + HIS] + out[2 * cut + HIS :]

    for copy in last:
        copy.wait()
    diag = []
    for c in range(FIELDS):
        total = jnp.zeros((HIS, LANES), f32)
        for a in range(4):
            i = c * 4 + a
            total += ref[i : i + 1, i : i + 1] * weight[a]
        diag.append(total)
    both = jnp.concatenate([sens] + diag, axis=0)
    field[...] = both
    up[...] = rim_rows(both, HIS - 2)
    low[...] = reorder(rim_rows(both, 0), perm[...], NN)


def group_place():
    return lax.axis_index("dom") % GROUP


def wall_kernel(blocks, owner, patch, *sums):
    rows = sums[0].shape[0]
    slot = (patch[...] // KEPT ^ group_place()) * rows + owner[...] * KEPT + patch[...] % KEPT
    top, rest = halves(blocks[...])
    both = jnp.concatenate([top, rest], axis=0).astype(bf16)
    for k in range(GROUP):
        out = mxu(one_hot(slot - k * rows, rows), both, NT)
        sums[k][...] = out[:, :LANES] + out[:, LANES:]


def looked_up(table, slots, lines):
    count = table.shape[0] // HIS
    n = slots.shape[1] // LANES
    rows = [[] for _ in range(count)]
    for k in range(n):
        here = slots[:, k * LANES : (k + 1) * LANES]
        high, lane = here >> 7, here & (LANES - 1)
        for f in range(count):
            got = jnp.zeros((8, LANES), f32)
            for h in lines:
                line = jnp.broadcast_to(table[f * HIS + h : f * HIS + h + 1], (8, LANES))
                picked = jnp.take_along_axis(line, lane, axis=1, mode="promise_in_bounds")
                got = jnp.where(high == h, picked, got)
            rows[f].append(got)
    return [jnp.concatenate(r, axis=1) for r in rows]


def apply_kernel(
    field, below, above, conn, stiff, perm, ref,
    base, scale, applied, up, low,
    *, chunk,
):
    shared = field[...] + rims(below[...], above[...], perm[...])
    cut = FIELDS * HIS
    sens, diag = shared[:cut], shared[cut:] + mass_shift
    over = relax / diag
    psi = over * sens
    base[...] = psi + over * (sens - mass_shift * psi)
    scale[...] = over

    index = lax.broadcasted_iota(jnp.int32, (24, 12), 0)
    pick = (index // 8 * 4 + index % 4) == lax.broadcasted_iota(jnp.int32, (24, 12), 1)
    pick = pick.astype(f32)
    wide = exact(exact(pick, ref[...], NN), pick, NT)
    half_of_row = lax.broadcasted_iota(jnp.int32, (24, 24), 0) // 4 % 2
    half_of_col = lax.broadcasted_iota(jnp.int32, (24, 24), 1) // 4 % 2
    wide = jnp.where(half_of_row == half_of_col, wide, 0.0)
    wide_top, wide_rest = halves(wide)
    wide = jnp.concatenate(
        [
            jnp.concatenate([wide_top, wide_top], axis=1),
            jnp.concatenate([wide_rest, wide_rest], axis=1),
        ],
        axis=0,
    ).astype(bf16)

    half = conn.shape[1] // 2
    total = jnp.zeros((cut, LANES), f32)
    for start in range(0, half, chunk):
        first = slice(start, start + chunk)
        second = slice(half + start, half + start + chunk)
        slots = jnp.concatenate([conn[:, first], conn[:, second]], axis=0)
        values = jnp.concatenate(looked_up(psi, slots, range(HIS)), axis=0)
        top, rest = halves(values)
        pushed = mxu(wide, jnp.concatenate([top, rest], axis=0).astype(bf16), NN)
        pushed = pushed[:24] + pushed[24:]
        in_first = lax.broadcasted_iota(jnp.int32, (8, chunk), 0) < 4
        weight = jnp.where(in_first, stiff[:, first], stiff[:, second])
        pushed = pushed * jnp.concatenate([weight] * FIELDS, axis=0)
        top, rest = halves(pushed)
        high, lane = slots >> 7, slots & (LANES - 1)
        for row in range(8):
            rows = [x[c * 8 + row : c * 8 + row + 1] for x in (top, rest) for c in range(FIELDS)]
            spread = placed(high[row : row + 1], rows)
            out = mxu(spread, one_hot(lane[row : row + 1], LANES), NT)
            total += out[:cut] + out[cut:]
    applied[...] = total
    up[...] = rim_rows(total, HIS - 2)
    low[...] = reorder(rim_rows(total, 0), perm[...], NN)


def patch_sums(values, owner, patch, owners):
    half = values[0].shape[1]
    parts = [halves(v) for v in values]
    total = jnp.zeros((owners, 24 * PATCH_DEV), f32)
    for k in range(2):
        cols = slice(k * half, (k + 1) * half)
        rows = [
            parts[c][p][4 * k + a : 4 * k + a + 1]
            for p in range(2)
            for c in range(FIELDS)
            for a in range(4)
        ]
        spread = placed(patch[:, cols], rows)
        total += mxu(one_hot(owner[:, cols], owners), spread, NT)
    return total[:, : 12 * PATCH_DEV] + total[:, 12 * PATCH_DEV :]


def wall_slots(conn):
    half = conn.shape[1] // 2
    return jnp.concatenate([conn[:, :half], conn[:, half:]], axis=0)


def local_kernel(base, scale, applied, conn, owner, patch, local, sums):
    psi = base[...] - scale[...] * applied[...]
    local[...] = psi
    values = looked_up(psi, wall_slots(conn), range(HIS))
    sums[:, : 12 * PATCH_DEV] = patch_sums(values, owner, patch, sums.shape[0])
    sums[:, 12 * PATCH_DEV :] = jnp.zeros((sums.shape[0], 4 * PATCH_DEV), f32)


def rim_kernel(
    local, scale, below, above, conn, owner, patch, perm, sums, *rest
):
    *pieces, adjoint, payload = rest
    change = -scale[...] * rims(below[...], above[...], perm[...])
    psi = local[...] + change
    for c in range(FIELDS):
        for h in range(HIS):
            adjoint[c : c + 1, h * LANES : (h + 1) * LANES] = psi[c * HIS + h : c * HIS + h + 1]
    values = looked_up(change, wall_slots(conn), (0, 1, HIS - 2, HIS - 1))
    owners = sums.shape[0]
    more = patch_sums(values, owner, patch, owners)
    total = sums[...] + jnp.concatenate([more, jnp.zeros((owners, 4 * PATCH_DEV), f32)], axis=1)
    kept = pieces[0][...]
    for piece in pieces[1:]:
        kept += piece[...]
    payload[:, :KEPT, :] = kept.reshape(owners, KEPT, LANES)
    payload[:, KEPT : KEPT + 1, :] = total[:, :LANES].reshape(owners, 1, LANES)
    payload[:, KEPT + 1 : KEPT + 2, :] = total[:, LANES:].reshape(owners, 1, LANES)
    payload[:, KEPT + 2 :, :] = jnp.zeros((owners, ROWS - KEPT - 2, LANES), f32)


def owner_kernel(got, w_adjoint, out):
    doms = lax.axis_size("dom")
    subs = got.shape[0] // doms
    by_dom = []
    for d in range(doms):
        total = got[d * subs]
        for s in range(1, subs):
            total += got[d * subs + s]
        by_dom.append(total)
    parts = []
    for g in range(GROUP):
        total = by_dom[g]
        for d in range(g + GROUP, doms, GROUP):
            total += by_dom[d]
        parts.append(total[:KEPT])
    everything = by_dom[0]
    for d in range(1, doms):
        everything += by_dom[d]
    shape = (PATCH_DEV, LANES)
    mine = lax.broadcasted_iota(jnp.int32, shape, 1) % PATCH_DEV == lax.broadcasted_iota(
        jnp.int32, shape, 0
    )
    spread = [
        jnp.where(mine, everything[KEPT + k : KEPT + k + 1], 0.0) for k in range(2)
    ]
    shape = (2 * LANES, w_adjoint.shape[0])
    rows = lax.broadcasted_iota(jnp.int32, shape, 0) // PATCH_DEV
    pick = (rows == lax.broadcasted_iota(jnp.int32, shape, 1)).astype(f32)
    weights = exact(pick, w_adjoint[...].astype(f32), NN)
    out[...] = jnp.concatenate(parts, axis=0) + exact(
        jnp.concatenate(spread, axis=1), weights, NN
    )


def params(flops, bytes_accessed, vmem=24):
    return dict(
        compiler_params=pltpu.CompilerParams(vmem_limit_bytes=vmem * 2**20),
        cost_estimate=pl.CostEstimate(
            flops=flops, bytes_accessed=bytes_accessed, transcendentals=0
        ),
    )


def whole(shape):
    return pl.BlockSpec(shape, lambda s: (0,) * len(shape))


def shape(*dims):
    return jax.ShapeDtypeStruct(dims, f32)


def front(walls, *fetched):
    trace, elements = fetched[0].shape
    quad, width = fetched[8].shape
    outs = [shape(2 * FIELDS * HIS, LANES), shape(6, RIM), shape(6, RIM), shape(width, walls)]
    copies = len(fetched) + 2 * (elements // walls - 1)
    return pl.pallas_call(
        functools.partial(front_kernel, walls=walls),
        in_specs=[pl.BlockSpec(memory_space=pl.ANY)] * len(fetched),
        out_shape=outs,
        scratch_shapes=[
            *(pltpu.VMEM(x.shape, x.dtype) for x in fetched),
            pltpu.SemaphoreType.DMA((copies,)),
        ],
        name="front",
        **params(4 * elements * trace * quad, 4 * elements * trace, FRONT_VMEM),
    )(*(pltpu.with_memory_space_constraint(x, pltpu.HBM) for x in fetched))


def apply(field, below, above, connect, stiff, perm, stiff_ref):
    elements = connect.shape[1]
    cut = FIELDS * HIS
    small = shape(cut, LANES)
    return pl.pallas_call(
        functools.partial(apply_kernel, chunk=512),
        out_shape=[small, small, small, shape(3, RIM), shape(3, RIM)],
        name="apply",
        **params(16 * elements * LANES * cut, 24 * elements),
    )(field, below, above, connect, stiff, perm, stiff_ref)


def exchanged(up, low):
    count = lax.axis_size("sub")
    below = lax.ppermute(up, "sub", [(i, (i + 1) % count) for i in range(count)])
    above = lax.ppermute(low, "sub", [(i, (i - 1) % count) for i in range(count)])
    return below, above


def per_device(
    adjoint_traces,
    primal_traces,
    jacobian,
    stiffness,
    connect,
    shared_perm,
    wall_owner,
    wall_patch,
    w_trace,
    w_state,
    w_node,
    w_block,
    w_adjoint,
    stiff_ref,
):
    walls = wall_owner.shape[0]
    devices = lax.axis_size("dom") * lax.axis_size("sub")
    width = w_block.shape[1]
    jac = jacobian.reshape(1, -1)
    stiff = stiffness.reshape(1, -1)
    owner = wall_owner.reshape(1, -1)
    patch = wall_patch.reshape(1, -1)
    perm = shared_perm.reshape(1, -1)
    field, up, low, blocks = front(
        walls, adjoint_traces, primal_traces, jac, stiff, connect,
        w_trace, w_state, w_node.T, w_block, perm, stiff_ref,
    )
    below, above = exchanged(up, low)

    pieces = pl.pallas_call(
        wall_kernel,
        out_shape=[shape(devices * KEPT, width)] * GROUP,
        name="walls",
        **params(4 * walls * width * devices * PATCH_DEV, 8 * walls * width),
    )(blocks, owner, patch)
    *pieces, below, above = lax.optimization_barrier((*pieces, below, above))
    doms = lax.axis_size("dom")
    pieces = [
        pieces[0],
        *(
            lax.ppermute(pieces[k], "dom", [(i, i ^ k) for i in range(doms)])
            for k in range(1, GROUP)
        ),
    ]

    small = shape(FIELDS * HIS, LANES)
    base, scale, applied, up, low = apply(
        field, below, above, connect, stiff, perm, stiff_ref
    )
    below, above = exchanged(up, low)

    conn_spec = pl.BlockSpec((4, walls), lambda s: (0, 0))
    local, sums = pl.pallas_call(
        local_kernel,
        grid=(1,),
        in_specs=[
            *[whole(small.shape)] * 3, conn_spec, whole(owner.shape), whole(patch.shape),
        ],
        out_specs=[whole(small.shape), whole((devices, 2 * LANES))],
        out_shape=[small, shape(devices, 2 * LANES)],
        name="local",
        **params(3000 * walls * LANES, 8 * devices * PATCH_DEV * width),
    )(base, scale, applied, connect, owner, patch)

    adjoint, payload = pl.pallas_call(
        rim_kernel,
        grid=(1,),
        in_specs=[
            *[whole(small.shape)] * 2, whole(below.shape), whole(above.shape), conn_spec,
            whole(owner.shape), whole(patch.shape), whole(perm.shape), whole(sums.shape),
            *[whole(pieces[0].shape)] * GROUP,
        ],
        out_specs=[whole((FIELDS, HIS * LANES)), whole((devices, ROWS, LANES))],
        out_shape=[shape(FIELDS, HIS * LANES), shape(devices, ROWS, LANES)],
        name="rims",
        **params(3000 * walls * LANES, 8 * devices * PATCH_DEV * width),
    )(local, scale, below, above, connect, owner, patch, perm, sums, *pieces)

    got = lax.all_to_all(payload, ("dom", "sub"), split_axis=0, concat_axis=0, tiled=True)
    grad = pl.pallas_call(
        owner_kernel,
        out_shape=shape(PATCH_DEV, width),
        name="owners",
        **params(10**6, 4 * devices * ROWS * width),
    )(got, w_adjoint)
    return (grad, adjoint)


def solution(mesh):
    both = ("dom", "sub")
    return jax.shard_map(
        per_device,
        mesh=mesh,
        in_specs=(
            P(None, both),
            P(None, both),
            P(both),
            P(both),
            P(None, both),
            P("dom", "sub", None),
            P(both, None),
            P(both),
            P(),
            P(),
            P(),
            P(),
            P(),
            P(),
        ),
        out_specs=(P(both, None), P(None, both)),
        check_vma=False,
    )
```

```python
import functools

import jax
import jax.numpy as jnp
from jax import lax
from jax.experimental import pallas as pl
from jax.experimental.pallas import tpu as pltpu
from jax.sharding import PartitionSpec as P

PATCH_DEV = 16
LANES = 128
HIS = 16
FIELDS = 3
RIM = 256
GROUP = 4
KEPT = PATCH_DEV // GROUP
FRONT_VMEM = 40
ROWS = KEPT + 2

mass_shift = 0.5
relax = 0.7

f32 = jnp.float32
bf16 = jnp.bfloat16

NN = (((1,), (0,)), ((), ()))
NT = (((1,), (1,)), ((), ()))


def mxu(a, b, dims):
    return lax.dot_general(a, b, dims, preferred_element_type=f32)


def exact(a, b, dims):
    return lax.dot_general(
        a, b, dims, preferred_element_type=f32, precision=lax.Precision.HIGHEST
    )


def halves(x):
    top = x.astype(bf16).astype(f32)
    return top, x - top


def one_hot(index_row, rows):
    shape = (rows, index_row.shape[1])
    wanted = jnp.broadcast_to(index_row.astype(jnp.int16), shape)
    hit = wanted == lax.broadcasted_iota(jnp.int16, shape, 0)
    return jnp.where(hit, jnp.ones(shape, bf16), jnp.zeros(shape, bf16))


def placed(index_row, value_rows):
    shape = (HIS, index_row.shape[1])
    wanted = jnp.broadcast_to(index_row.astype(jnp.int16), shape)
    hit = wanted == lax.broadcasted_iota(jnp.int16, shape, 0)
    zero = jnp.zeros(shape, bf16)
    return jnp.concatenate(
        [jnp.where(hit, jnp.broadcast_to(v, shape).astype(bf16), zero) for v in value_rows], axis=0
    )


def rim_rows(field, first):
    count = field.shape[0] // HIS
    parts = [
        jnp.concatenate([field[f * HIS + first + k : f * HIS + first + k + 1] for f in range(count)], 0)
        for k in range(2)
    ]
    return jnp.concatenate(parts, axis=1)


def reorder(rows, perm_row, dims):
    count = rows.shape[0]
    table = one_hot(perm_row, RIM)
    first, rest = halves(rows)
    second, third = halves(rest)
    pad = jnp.zeros((-count % 8, RIM), f32)
    stack = jnp.concatenate([first, pad, second, pad, third, pad], axis=0).astype(bf16)
    out = mxu(stack, table, dims)
    step = count + (-count % 8)
    return out[:count] + out[step : step + count] + out[2 * step : 2 * step + count]


def rims(below, above, perm_row):
    count = below.shape[0]
    place = lax.axis_index("sub")
    last = lax.axis_size("sub") - 1
    below = jnp.where(place == 0, 0.0, below)
    above = jnp.where(place == last, 0.0, above)
    low = reorder(below, perm_row, NT)
    parts = []
    for f in range(count):
        parts += [
            low[f : f + 1, :LANES],
            low[f : f + 1, LANES:],
            jnp.zeros((HIS - 4, LANES), f32),
            above[f : f + 1, :LANES],
            above[f : f + 1, LANES:],
        ]
    return jnp.concatenate(parts, axis=0)


def front_kernel(*refs, walls):
    sources, (field, up, low, blocks), held, sems = refs[:11], refs[11:15], refs[15:26], refs[26]
    traces, states, jac, stiff, conn, w_trace, w_state, w_node, w_block, perm, ref = held
    cuts = [0, walls // 4, *range(walls, traces.shape[1] + 1, walls)]
    spans = [slice(p, q) for p, q in zip(cuts, cuts[1:])]
    copies = []

    def fetch(k, span=None):
        source, target = sources[k], held[k]
        if span is not None:
            source, target = source.at[:, span], target.at[:, span]
        copy = pltpu.make_async_copy(source, target, sems.at[len(copies)])
        copy.start()
        copies.append(copy)
        return copy

    weights = [fetch(k) for k in (5, 6, 7, 8)]
    first = [fetch(0, spans[0]), fetch(1, spans[0]), fetch(2)]
    small = [fetch(k) for k in (3, 4)]
    later = [[fetch(0, span), fetch(1, span)] for span in spans[1:]]
    last = [fetch(k) for k in (9, 10)]
    for copy in weights:
        copy.wait()
    trace_t = w_trace[...].astype(f32).T.astype(bf16)
    state_t = w_state[...].astype(f32).T.astype(bf16)
    pad = jnp.zeros((4, w_node.shape[1]), f32)
    node_t = jnp.concatenate([w_node[...].astype(f32), pad], axis=0).astype(bf16)
    block_t = w_block[...].astype(f32).T.astype(bf16)
    cut = FIELDS * HIS
    sums = [jnp.zeros((LANES, 2 * (cut + HIS)), f32) for _ in range(4)]
    for s, span in enumerate(spans):
        for copy in first if s == 0 else later[s - 1]:
            copy.wait()
        upsilon = mxu(trace_t, traces[:, span], NN)
        tangent = mxu(state_t, states[:, span], NN)
        product = (jac[:, span] * upsilon * tangent).astype(bf16)
        terms = mxu(node_t, product, NN)
        if s < 2:
            blocks[:, span] = mxu(block_t, product, NN)
        if s == 0:
            for copy in small:
                copy.wait()
        top, rest = halves(terms)
        stiff_top, stiff_rest = halves(stiff[:, span])
        slots = conn[:, span]
        high, lane = slots >> 7, slots & (LANES - 1)
        for a in range(4):
            rows = [top[c * 4 + a : c * 4 + a + 1] for c in range(FIELDS)] + [stiff_top]
            rows += [rest[c * 4 + a : c * 4 + a + 1] for c in range(FIELDS)] + [stiff_rest]
            spread = placed(high[a : a + 1], rows)
            sums[a] += mxu(one_hot(lane[a : a + 1], LANES), spread, NT)

    for copy in last:
        copy.wait()
    sums = [x.T for x in sums]
    sums = [x[: cut + HIS] + x[cut + HIS :] for x in sums]
    sens = sums[0][:cut] + sums[1][:cut] + sums[2][:cut] + sums[3][:cut]
    diag = []
    for c in range(FIELDS):
        total = jnp.zeros((HIS, LANES), f32)
        for a in range(4):
            i = c * 4 + a
            total += ref[i : i + 1, i : i + 1] * sums[a][cut:]
        diag.append(total)
    both = jnp.concatenate([sens] + diag, axis=0)
    field[...] = both
    up[...] = rim_rows(both, HIS - 2)
    low[...] = reorder(rim_rows(both, 0), perm[...], NN)


def group_place():
    return lax.axis_index("dom") % GROUP


def wall_kernel(blocks, owner, patch, *sums):
    rows = sums[0].shape[0]
    slot = (patch[...] // KEPT ^ group_place()) * rows + owner[...] * KEPT + patch[...] % KEPT
    top, rest = halves(blocks[...])
    both = jnp.concatenate([top, rest], axis=0).astype(bf16)
    for k in range(GROUP):
        out = mxu(one_hot(slot - k * rows, rows), both, NT)
        sums[k][...] = out[:, :LANES] + out[:, LANES:]


def looked_up(table, slots, lines):
    count = table.shape[0] // HIS
    n = slots.shape[1] // LANES
    rows = [[] for _ in range(count)]
    for k in range(n):
        here = slots[:, k * LANES : (k + 1) * LANES]
        high, lane = here >> 7, here & (LANES - 1)
        for f in range(count):
            got = jnp.zeros((8, LANES), f32)
            for h in lines:
                line = jnp.broadcast_to(table[f * HIS + h : f * HIS + h + 1], (8, LANES))
                picked = jnp.take_along_axis(line, lane, axis=1, mode="promise_in_bounds")
                got = jnp.where(high == h, picked, got)
            rows[f].append(got)
    return [jnp.concatenate(r, axis=1) for r in rows]


def apply_kernel(
    field, below, above, conn, stiff, perm, ref,
    base, scale, applied, up, low,
    *, chunk,
):
    shared = field[...] + rims(below[...], above[...], perm[...])
    cut = FIELDS * HIS
    sens, diag = shared[:cut], shared[cut:] + mass_shift
    over = relax / diag
    psi = over * sens
    base[...] = psi + over * (sens - mass_shift * psi)
    scale[...] = over

    index = lax.broadcasted_iota(jnp.int32, (24, 12), 0)
    pick = (index // 8 * 4 + index % 4) == lax.broadcasted_iota(jnp.int32, (24, 12), 1)
    pick = pick.astype(f32)
    wide = exact(exact(pick, ref[...], NN), pick, NT)
    half_of_row = lax.broadcasted_iota(jnp.int32, (24, 24), 0) // 4 % 2
    half_of_col = lax.broadcasted_iota(jnp.int32, (24, 24), 1) // 4 % 2
    wide = jnp.where(half_of_row == half_of_col, wide, 0.0)
    wide_top, wide_rest = halves(wide)
    wide = jnp.concatenate(
        [
            jnp.concatenate([wide_top, wide_top], axis=1),
            jnp.concatenate([wide_rest, wide_rest], axis=1),
        ],
        axis=0,
    ).astype(bf16)

    half = conn.shape[1] // 2
    total = jnp.zeros((cut, LANES), f32)
    for start in range(0, half, chunk):
        first = slice(start, start + chunk)
        second = slice(half + start, half + start + chunk)
        slots = jnp.concatenate([conn[:, first], conn[:, second]], axis=0)
        values = jnp.concatenate(looked_up(psi, slots, range(HIS)), axis=0)
        top, rest = halves(values)
        pushed = mxu(wide, jnp.concatenate([top, rest], axis=0).astype(bf16), NN)
        pushed = pushed[:24] + pushed[24:]
        in_first = lax.broadcasted_iota(jnp.int32, (8, chunk), 0) < 4
        weight = jnp.where(in_first, stiff[:, first], stiff[:, second])
        pushed = pushed * jnp.concatenate([weight] * FIELDS, axis=0)
        top, rest = halves(pushed)
        high, lane = slots >> 7, slots & (LANES - 1)
        for row in range(8):
            rows = [x[c * 8 + row : c * 8 + row + 1] for x in (top, rest) for c in range(FIELDS)]
            spread = placed(high[row : row + 1], rows)
            out = mxu(spread, one_hot(lane[row : row + 1], LANES), NT)
            total += out[:cut] + out[cut:]
    applied[...] = total
    up[...] = rim_rows(total, HIS - 2)
    low[...] = reorder(rim_rows(total, 0), perm[...], NN)


def patch_sums(values, owner, patch, owners):
    half = values[0].shape[1]
    parts = [halves(v) for v in values]
    total = jnp.zeros((owners, 24 * PATCH_DEV), f32)
    for k in range(2):
        cols = slice(k * half, (k + 1) * half)
        rows = [
            parts[c][p][4 * k + a : 4 * k + a + 1]
            for p in range(2)
            for c in range(FIELDS)
            for a in range(4)
        ]
        spread = placed(patch[:, cols], rows)
        total += mxu(one_hot(owner[:, cols], owners), spread, NT)
    return total[:, : 12 * PATCH_DEV] + total[:, 12 * PATCH_DEV :]


def wall_slots(conn):
    half = conn.shape[1] // 2
    return jnp.concatenate([conn[:, :half], conn[:, half:]], axis=0)


def local_kernel(base, scale, applied, conn, owner, patch, local, sums):
    psi = base[...] - scale[...] * applied[...]
    local[...] = psi
    values = looked_up(psi, wall_slots(conn), range(HIS))
    sums[:, : 12 * PATCH_DEV] = patch_sums(values, owner, patch, sums.shape[0])
    sums[:, 12 * PATCH_DEV :] = jnp.zeros((sums.shape[0], 4 * PATCH_DEV), f32)


def rim_kernel(
    local, scale, below, above, conn, owner, patch, perm, sums, *rest
):
    *pieces, adjoint, payload = rest
    change = -scale[...] * rims(below[...], above[...], perm[...])
    psi = local[...] + change
    for c in range(FIELDS):
        for h in range(HIS):
            adjoint[c : c + 1, h * LANES : (h + 1) * LANES] = psi[c * HIS + h : c * HIS + h + 1]
    values = looked_up(change, wall_slots(conn), (0, 1, HIS - 2, HIS - 1))
    owners = sums.shape[0]
    more = patch_sums(values, owner, patch, owners)
    total = sums[...] + jnp.concatenate([more, jnp.zeros((owners, 4 * PATCH_DEV), f32)], axis=1)
    kept = pieces[0][...]
    for piece in pieces[1:]:
        kept += piece[...]
    kept = kept.reshape(owners, KEPT, LANES)
    for k in range(2):
        rows = [kept[:, r, :] for r in range(k, KEPT, 2)] + [total[:, k * LANES : (k + 1) * LANES]]
        payload[:, k : k + 1, :] = jnp.concatenate(rows, axis=1).reshape(owners, 1, ROWS // 2 * LANES)


def owner_kernel(got, w_adjoint, out):
    doms = lax.axis_size("dom")
    subs = got.shape[0] // doms
    by_dom = []
    for d in range(doms):
        total = got[d * subs]
        for s in range(1, subs):
            total += got[d * subs + s]
        by_dom.append(total)
    parts = []
    for g in range(GROUP):
        total = by_dom[g]
        for d in range(g + GROUP, doms, GROUP):
            total += by_dom[d]
        parts += [total[r % 2 : r % 2 + 1, r // 2 * LANES : (r // 2 + 1) * LANES] for r in range(KEPT)]
    everything = by_dom[0]
    for d in range(1, doms):
        everything += by_dom[d]
    everything = everything[:, KEPT // 2 * LANES :]
    shape = (PATCH_DEV, LANES)
    mine = lax.broadcasted_iota(jnp.int32, shape, 1) % PATCH_DEV == lax.broadcasted_iota(
        jnp.int32, shape, 0
    )
    spread = [
        jnp.where(mine, everything[k : k + 1], 0.0) for k in range(2)
    ]
    shape = (2 * LANES, w_adjoint.shape[0])
    rows = lax.broadcasted_iota(jnp.int32, shape, 0) // PATCH_DEV
    pick = (rows == lax.broadcasted_iota(jnp.int32, shape, 1)).astype(f32)
    weights = exact(pick, w_adjoint[...].astype(f32), NN)
    out[...] = jnp.concatenate(parts, axis=0) + exact(
        jnp.concatenate(spread, axis=1), weights, NN
    )


def params(flops, bytes_accessed, vmem=24):
    return dict(
        compiler_params=pltpu.CompilerParams(vmem_limit_bytes=vmem * 2**20),
        cost_estimate=pl.CostEstimate(
            flops=flops, bytes_accessed=bytes_accessed, transcendentals=0
        ),
    )


def whole(shape):
    return pl.BlockSpec(shape, lambda s: (0,) * len(shape))


def shape(*dims):
    return jax.ShapeDtypeStruct(dims, f32)


def front(walls, *fetched):
    trace, elements = fetched[0].shape
    quad, width = fetched[8].shape
    outs = [shape(2 * FIELDS * HIS, LANES), shape(6, RIM), shape(6, RIM), shape(width, walls)]
    copies = len(fetched) + 2 * (elements // walls)
    return pl.pallas_call(
        functools.partial(front_kernel, walls=walls),
        in_specs=[pl.BlockSpec(memory_space=pl.ANY)] * len(fetched),
        out_shape=outs,
        scratch_shapes=[
            *(pltpu.VMEM(x.shape, x.dtype) for x in fetched),
            pltpu.SemaphoreType.DMA((copies,)),
        ],
        name="front",
        **params(4 * elements * trace * quad, 4 * elements * trace, FRONT_VMEM),
    )(*(pltpu.with_memory_space_constraint(x, pltpu.HBM) for x in fetched))


def apply(field, below, above, connect, stiff, perm, stiff_ref):
    elements = connect.shape[1]
    cut = FIELDS * HIS
    small = shape(cut, LANES)
    return pl.pallas_call(
        functools.partial(apply_kernel, chunk=512),
        out_shape=[small, small, small, shape(3, RIM), shape(3, RIM)],
        name="apply",
        **params(16 * elements * LANES * cut, 24 * elements),
    )(field, below, above, connect, stiff, perm, stiff_ref)


def exchanged(up, low):
    count = lax.axis_size("sub")
    below = lax.ppermute(up, "sub", [(i, (i + 1) % count) for i in range(count)])
    above = lax.ppermute(low, "sub", [(i, (i - 1) % count) for i in range(count)])
    return below, above


def per_device(
    adjoint_traces,
    primal_traces,
    jacobian,
    stiffness,
    connect,
    shared_perm,
    wall_owner,
    wall_patch,
    w_trace,
    w_state,
    w_node,
    w_block,
    w_adjoint,
    stiff_ref,
):
    walls = wall_owner.shape[0]
    devices = lax.axis_size("dom") * lax.axis_size("sub")
    width = w_block.shape[1]
    jac = jacobian.reshape(1, -1)
    stiff = stiffness.reshape(1, -1)
    owner = wall_owner.reshape(1, -1)
    patch = wall_patch.reshape(1, -1)
    perm = shared_perm.reshape(1, -1)
    field, up, low, blocks = front(
        walls, adjoint_traces, primal_traces, jac, stiff, connect,
        w_trace, w_state, w_node.T, w_block, perm, stiff_ref,
    )
    below, above = exchanged(up, low)

    pieces = pl.pallas_call(
        wall_kernel,
        out_shape=[shape(devices * KEPT, width)] * GROUP,
        name="walls",
        **params(4 * walls * width * devices * PATCH_DEV, 8 * walls * width),
    )(blocks, owner, patch)
    *pieces, below, above = lax.optimization_barrier((*pieces, below, above))
    doms = lax.axis_size("dom")
    pieces = [
        pieces[0],
        *(
            lax.ppermute(pieces[k], "dom", [(i, i ^ k) for i in range(doms)])
            for k in range(1, GROUP)
        ),
    ]

    small = shape(FIELDS * HIS, LANES)
    base, scale, applied, up, low = apply(
        field, below, above, connect, stiff, perm, stiff_ref
    )
    below, above = exchanged(up, low)

    conn_spec = pl.BlockSpec((4, walls), lambda s: (0, 0))
    local, sums = pl.pallas_call(
        local_kernel,
        grid=(1,),
        in_specs=[
            *[whole(small.shape)] * 3, conn_spec, whole(owner.shape), whole(patch.shape),
        ],
        out_specs=[whole(small.shape), whole((devices, 2 * LANES))],
        out_shape=[small, shape(devices, 2 * LANES)],
        name="local",
        **params(3000 * walls * LANES, 8 * devices * PATCH_DEV * width),
    )(base, scale, applied, connect, owner, patch)

    adjoint, payload = pl.pallas_call(
        rim_kernel,
        grid=(1,),
        in_specs=[
            *[whole(small.shape)] * 2, whole(below.shape), whole(above.shape), conn_spec,
            whole(owner.shape), whole(patch.shape), whole(perm.shape), whole(sums.shape),
            *[whole(pieces[0].shape)] * GROUP,
        ],
        out_specs=[whole((FIELDS, HIS * LANES)), whole((devices, 2, ROWS // 2 * LANES))],
        out_shape=[shape(FIELDS, HIS * LANES), shape(devices, 2, ROWS // 2 * LANES)],
        name="rims",
        **params(3000 * walls * LANES, 8 * devices * PATCH_DEV * width),
    )(local, scale, below, above, connect, owner, patch, perm, sums, *pieces)

    got = lax.all_to_all(payload, ("dom", "sub"), split_axis=0, concat_axis=0, tiled=True)
    grad = pl.pallas_call(
        owner_kernel,
        out_shape=shape(PATCH_DEV, width),
        name="owners",
        **params(10**6, 4 * devices * ROWS * width),
    )(got, w_adjoint)
    return (grad, adjoint)


def solution(mesh):
    both = ("dom", "sub")
    return jax.shard_map(
        per_device,
        mesh=mesh,
        in_specs=(
            P(None, both),
            P(None, both),
            P(both),
            P(both),
            P(None, both),
            P("dom", "sub", None),
            P(both, None),
            P(both),
            P(),
            P(),
            P(),
            P(),
            P(),
            P(),
        ),
        out_specs=(P(both, None), P(None, both)),
        check_vma=False,
    )
```

```python
import functools

import jax
import jax.numpy as jnp
from jax import lax
from jax.experimental import pallas as pl
from jax.experimental.pallas import tpu as pltpu
from jax.sharding import PartitionSpec as P

PATCH_DEV = 16
LANES = 128
HIS = 16
FIELDS = 3
RIM = 256
PIECES = 8
GROUP = 2
KEPT = PATCH_DEV // GROUP
FRONT_VMEM = 40
ROWS = KEPT + 2

mass_shift = 0.5
relax = 0.7

f32 = jnp.float32
bf16 = jnp.bfloat16

NN = (((1,), (0,)), ((), ()))
NT = (((1,), (1,)), ((), ()))


def mxu(a, b, dims):
    return lax.dot_general(a, b, dims, preferred_element_type=f32)


def exact(a, b, dims):
    return lax.dot_general(
        a, b, dims, preferred_element_type=f32, precision=lax.Precision.HIGHEST
    )


def halves(x):
    top = x.astype(bf16).astype(f32)
    return top, x - top


def one_hot(index_row, rows):
    shape = (rows, index_row.shape[1])
    wanted = jnp.broadcast_to(index_row.astype(jnp.int16), shape)
    hit = wanted == lax.broadcasted_iota(jnp.int16, shape, 0)
    return jnp.where(hit, jnp.ones(shape, bf16), jnp.zeros(shape, bf16))


def placed(index_row, value_rows):
    shape = (HIS, index_row.shape[1])
    wanted = jnp.broadcast_to(index_row.astype(jnp.int16), shape)
    hit = wanted == lax.broadcasted_iota(jnp.int16, shape, 0)
    zero = jnp.zeros(shape, bf16)
    return jnp.concatenate(
        [jnp.where(hit, jnp.broadcast_to(v, shape).astype(bf16), zero) for v in value_rows], axis=0
    )


def rim_rows(field, first):
    count = field.shape[0] // HIS
    parts = [
        jnp.concatenate([field[f * HIS + first + k : f * HIS + first + k + 1] for f in range(count)], 0)
        for k in range(2)
    ]
    return jnp.concatenate(parts, axis=1)


def reorder(rows, perm_row, dims):
    count = rows.shape[0]
    table = one_hot(perm_row, RIM)
    first, rest = halves(rows)
    second, third = halves(rest)
    pad = jnp.zeros((-count % 8, RIM), f32)
    stack = jnp.concatenate([first, pad, second, pad, third, pad], axis=0).astype(bf16)
    out = mxu(stack, table, dims)
    step = count + (-count % 8)
    return out[:count] + out[step : step + count] + out[2 * step : 2 * step + count]


def rims(below, above, perm_row):
    count = below.shape[0]
    place = lax.axis_index("sub")
    last = lax.axis_size("sub") - 1
    below = jnp.where(place == 0, 0.0, below)
    above = jnp.where(place == last, 0.0, above)
    low = reorder(below, perm_row, NT)
    parts = []
    for f in range(count):
        parts += [
            low[f : f + 1, :LANES],
            low[f : f + 1, LANES:],
            jnp.zeros((HIS - 4, LANES), f32),
            above[f : f + 1, :LANES],
            above[f : f + 1, LANES:],
        ]
    return jnp.concatenate(parts, axis=0)


def write_message(message, rims, perm, conn, owner, patch):
    message[:8] = jnp.concatenate([rims, perm[...].astype(f32), jnp.zeros((1, RIM), f32)], axis=0)
    for i in range(PIECES):
        cols = slice(i * RIM, (i + 1) * RIM)
        message[8 + 4 * i : 12 + 4 * i] = conn[:, cols].astype(f32)
        target = owner[:, cols] * PATCH_DEV + patch[:, cols]
        message[8 + 4 * PIECES + i : 9 + 4 * PIECES + i] = target.astype(f32)


def read_message(message):
    pairs = range(PIECES // 2)
    slots = jnp.concatenate([message[8 + 8 * j : 16 + 8 * j] for j in pairs], axis=1)
    first = 8 + 4 * PIECES
    targets = [
        jnp.concatenate([message[first + 2 * j + k : first + 2 * j + k + 1] for j in pairs], axis=1)
        for k in range(2)
    ]
    return slots.astype(jnp.int32), [x.astype(jnp.int32) for x in targets]


def front_kernel(*refs, walls):
    count = (len(refs) - 5) // 2
    sources, (field, up, low, blocks), held = refs[:count], refs[count : count + 4], refs[count + 4 : -1]
    sems = refs[-1]
    traces, states, jac, stiff, conn, w_trace, w_state, w_node, w_block, perm, ref, owner, patch = held
    cuts = [0, walls // 4, *range(walls, traces.shape[1] + 1, walls)]
    spans = [slice(p, q) for p, q in zip(cuts, cuts[1:])]
    copies = []

    def fetch(k, span=None):
        source, target = sources[k], held[k]
        if span is not None:
            source, target = source.at[:, span], target.at[:, span]
        copy = pltpu.make_async_copy(source, target, sems.at[len(copies)])
        copy.start()
        copies.append(copy)
        return copy

    weights = [fetch(k) for k in (5, 6, 7, 8)]
    first = [fetch(0, spans[0]), fetch(1, spans[0]), fetch(2)]
    small = [fetch(k) for k in (3, 4)]
    later = [[fetch(0, span), fetch(1, span)] for span in spans[1:]]
    last = [fetch(k) for k in (9, 10, 11, 12)]
    for copy in weights:
        copy.wait()
    trace_t = w_trace[...].astype(f32).T.astype(bf16)
    state_t = w_state[...].astype(f32).T.astype(bf16)
    pad = jnp.zeros((4, w_node.shape[1]), f32)
    node_t = jnp.concatenate([w_node[...].astype(f32), pad], axis=0).astype(bf16)
    block_t = w_block[...].astype(f32).T.astype(bf16)
    cut = FIELDS * HIS
    sums = [jnp.zeros((LANES, 2 * (cut + HIS)), f32) for _ in range(4)]
    for s, span in enumerate(spans):
        for copy in first if s == 0 else later[s - 1]:
            copy.wait()
        upsilon = mxu(trace_t, traces[:, span], NN)
        tangent = mxu(state_t, states[:, span], NN)
        product = (jac[:, span] * upsilon * tangent).astype(bf16)
        terms = mxu(node_t, product, NN)
        if s < 2:
            blocks[:, span] = mxu(block_t, product, NN)
        if s == 0:
            for copy in small:
                copy.wait()
        top, rest = halves(terms)
        stiff_top, stiff_rest = halves(stiff[:, span])
        slots = conn[:, span]
        high, lane = slots >> 7, slots & (LANES - 1)
        for a in range(4):
            rows = [top[c * 4 + a : c * 4 + a + 1] for c in range(FIELDS)] + [stiff_top]
            rows += [rest[c * 4 + a : c * 4 + a + 1] for c in range(FIELDS)] + [stiff_rest]
            spread = placed(high[a : a + 1], rows)
            sums[a] += mxu(one_hot(lane[a : a + 1], LANES), spread, NT)

    for copy in last:
        copy.wait()
    sums = [x.T for x in sums]
    sums = [x[: cut + HIS] + x[cut + HIS :] for x in sums]
    sens = sums[0][:cut] + sums[1][:cut] + sums[2][:cut] + sums[3][:cut]
    diag = []
    for c in range(FIELDS):
        total = jnp.zeros((HIS, LANES), f32)
        for a in range(4):
            i = c * 4 + a
            total += ref[i : i + 1, i : i + 1] * sums[a][cut:]
        diag.append(total)
    both = jnp.concatenate([sens] + diag, axis=0)
    field[...] = both
    write_message(up, rim_rows(both, HIS - 2), perm, conn, owner, patch)
    write_message(low, reorder(rim_rows(both, 0), perm[...], NN), perm, conn, owner, patch)


def group_place():
    return lax.axis_index("dom") % GROUP


def wall_kernel(blocks, owner, patch, *sums):
    rows = sums[0].shape[0]
    owners = rows // KEPT
    slot = (patch[...] // KEPT ^ group_place()) * rows + patch[...] % KEPT * owners + owner[...]
    top, rest = halves(blocks[...])
    both = jnp.concatenate([top, rest], axis=0).astype(bf16)
    for k in range(GROUP):
        out = mxu(one_hot(slot - k * rows, rows), both, NT)
        sums[k][...] = out[:, :LANES] + out[:, LANES:]


def all_lines(table):
    return [[(h, table[f * HIS + h : f * HIS + h + 1]) for h in range(HIS)] for f in range(FIELDS)]


def rim_lines(rims, first):
    return [
        [(first + k, rims[f : f + 1, k * LANES : (k + 1) * LANES]) for k in range(2)]
        for f in range(FIELDS)
    ]


def looked_up(table, slots):
    n = slots.shape[1] // LANES
    rows = [[] for _ in table]
    for k in range(n):
        here = slots[:, k * LANES : (k + 1) * LANES]
        high, lane = here >> 7, here & (LANES - 1)
        for f, lines in enumerate(table):
            got = jnp.zeros((8, LANES), f32)
            for h, line in lines:
                line = jnp.broadcast_to(line, (8, LANES))
                picked = jnp.take_along_axis(line, lane, axis=1, mode="promise_in_bounds")
                got = jnp.where(high == h, picked, got)
            rows[f].append(got)
    return [jnp.concatenate(r, axis=1) for r in rows]


def apply_kernel(
    field, below, above, conn, stiff, perm, ref,
    base, scale, applied, up, low,
    *, chunk,
):
    shared = field[...] + rims(below[:6], above[:6], perm[...])
    cut = FIELDS * HIS
    sens, diag = shared[:cut], shared[cut:] + mass_shift
    over = relax / diag
    psi = over * sens
    base[...] = psi + over * (sens - mass_shift * psi)
    scale[...] = over

    index = lax.broadcasted_iota(jnp.int32, (24, 12), 0)
    pick = (index // 8 * 4 + index % 4) == lax.broadcasted_iota(jnp.int32, (24, 12), 1)
    pick = pick.astype(f32)
    wide = exact(exact(pick, ref[...], NN), pick, NT)
    half_of_row = lax.broadcasted_iota(jnp.int32, (24, 24), 0) // 4 % 2
    half_of_col = lax.broadcasted_iota(jnp.int32, (24, 24), 1) // 4 % 2
    wide = jnp.where(half_of_row == half_of_col, wide, 0.0)
    wide_top, wide_rest = halves(wide)
    wide = jnp.concatenate(
        [
            jnp.concatenate([wide_top, wide_top], axis=1),
            jnp.concatenate([wide_rest, wide_rest], axis=1),
        ],
        axis=0,
    ).astype(bf16)

    half = conn.shape[1] // 2
    total = jnp.zeros((cut, LANES), f32)
    for start in range(0, half, chunk):
        first = slice(start, start + chunk)
        second = slice(half + start, half + start + chunk)
        slots = jnp.concatenate([conn[:, first], conn[:, second]], axis=0)
        values = jnp.concatenate(looked_up(all_lines(psi), slots), axis=0)
        top, rest = halves(values)
        pushed = mxu(wide, jnp.concatenate([top, rest], axis=0).astype(bf16), NN)
        pushed = pushed[:24] + pushed[24:]
        in_first = lax.broadcasted_iota(jnp.int32, (8, chunk), 0) < 4
        weight = jnp.where(in_first, stiff[:, first], stiff[:, second])
        pushed = pushed * jnp.concatenate([weight] * FIELDS, axis=0)
        top, rest = halves(pushed)
        high, lane = slots >> 7, slots & (LANES - 1)
        for row in range(8):
            rows = [x[c * 8 + row : c * 8 + row + 1] for x in (top, rest) for c in range(FIELDS)]
            spread = placed(high[row : row + 1], rows)
            out = mxu(spread, one_hot(lane[row : row + 1], LANES), NT)
            total += out[:cut] + out[cut:]
    applied[...] = total
    up[...] = rim_rows(total, HIS - 2)
    low[...] = reorder(rim_rows(total, 0), perm[...], NN)


def patch_sums(values, targets, owners):
    parts = [halves(v) for v in values]
    total = jnp.zeros((owners, 24 * PATCH_DEV), f32)
    for k, target in enumerate(targets):
        rows = [
            parts[c][p][4 * k + a : 4 * k + a + 1]
            for p in range(2)
            for c in range(FIELDS)
            for a in range(4)
        ]
        spread = placed(target % PATCH_DEV, rows)
        total += mxu(one_hot(target // PATCH_DEV, owners), spread, NT)
    return total[:, : 12 * PATCH_DEV] + total[:, 12 * PATCH_DEV :]


def sums_kernel(base, scale, applied, below, above, conn, owner, patch, perm, *rest):
    *pieces, payload = rest
    owners = payload.shape[0]
    change = scale[...] * applied[...]
    psi = base[...] - change
    half = conn.shape[1] // 2
    slots = jnp.concatenate([conn[:, :half], conn[:, half:]], axis=0)
    target = owner[...] * PATCH_DEV + patch[...]
    values = looked_up(all_lines(psi), slots)
    total = patch_sums(values, [target[:, :half], target[:, half:]], owners)

    place = lax.axis_index("sub")
    last = lax.axis_size("sub") - 1
    lower = reorder(rim_rows(-change, 0), perm[...], NN)
    lower = jnp.where(place == 0, 0.0, lower)
    slots, targets = read_message(below)
    total += patch_sums(looked_up(rim_lines(lower, HIS - 2), slots), targets, owners)
    upper = reorder(rim_rows(-change, HIS - 2), above[6:7].astype(jnp.int32), NT)
    upper = jnp.where(place == last, 0.0, upper)
    slots, targets = read_message(above)
    total += patch_sums(looked_up(rim_lines(upper, 0), slots), targets, owners)

    total = jnp.concatenate([total, jnp.zeros((owners, 4 * PATCH_DEV), f32)], axis=1)
    kept = pieces[0][...]
    for piece in pieces[1:]:
        kept += piece[...]
    for k in range(2):
        rows = [kept[r * owners : (r + 1) * owners] for r in range(k, KEPT, 2)]
        rows.append(total[:, k * LANES : (k + 1) * LANES])
        payload[:, k : k + 1, :] = jnp.concatenate(rows, axis=1).reshape(owners, 1, ROWS // 2 * LANES)


def adjoint_kernel(base, scale, applied, below, above, perm, adjoint):
    psi = base[...] - scale[...] * (applied[...] + rims(below[...], above[...], perm[...]))
    for c in range(FIELDS):
        for h in range(HIS):
            adjoint[c : c + 1, h * LANES : (h + 1) * LANES] = psi[c * HIS + h : c * HIS + h + 1]


def owner_kernel(got, w_adjoint, out):
    doms = lax.axis_size("dom")
    subs = got.shape[0] // doms
    by_dom = []
    for d in range(doms):
        total = got[d * subs]
        for s in range(1, subs):
            total += got[d * subs + s]
        by_dom.append(total)
    parts = []
    for g in range(GROUP):
        total = by_dom[g]
        for d in range(g + GROUP, doms, GROUP):
            total += by_dom[d]
        parts += [total[r % 2 : r % 2 + 1, r // 2 * LANES : (r // 2 + 1) * LANES] for r in range(KEPT)]
    everything = by_dom[0]
    for d in range(1, doms):
        everything += by_dom[d]
    everything = everything[:, KEPT // 2 * LANES :]
    shape = (PATCH_DEV, LANES)
    mine = lax.broadcasted_iota(jnp.int32, shape, 1) % PATCH_DEV == lax.broadcasted_iota(
        jnp.int32, shape, 0
    )
    spread = [
        jnp.where(mine, everything[k : k + 1], 0.0) for k in range(2)
    ]
    shape = (2 * LANES, w_adjoint.shape[0])
    rows = lax.broadcasted_iota(jnp.int32, shape, 0) // PATCH_DEV
    pick = (rows == lax.broadcasted_iota(jnp.int32, shape, 1)).astype(f32)
    weights = exact(pick, w_adjoint[...].astype(f32), NN)
    out[...] = jnp.concatenate(parts, axis=0) + exact(
        jnp.concatenate(spread, axis=1), weights, NN
    )


def params(flops, bytes_accessed, vmem=24):
    return dict(
        compiler_params=pltpu.CompilerParams(vmem_limit_bytes=vmem * 2**20),
        cost_estimate=pl.CostEstimate(
            flops=flops, bytes_accessed=bytes_accessed, transcendentals=0
        ),
    )


def whole(shape):
    return pl.BlockSpec(shape, lambda s: (0,) * len(shape))


def shape(*dims):
    return jax.ShapeDtypeStruct(dims, f32)


def front(walls, *fetched):
    trace, elements = fetched[0].shape
    quad, width = fetched[8].shape
    message = shape(8 + 5 * PIECES, RIM)
    outs = [shape(2 * FIELDS * HIS, LANES), message, message, shape(width, walls)]
    copies = len(fetched) + 2 * (elements // walls)
    return pl.pallas_call(
        functools.partial(front_kernel, walls=walls),
        in_specs=[pl.BlockSpec(memory_space=pl.ANY)] * len(fetched),
        out_shape=outs,
        scratch_shapes=[
            *(pltpu.VMEM(x.shape, x.dtype) for x in fetched),
            pltpu.SemaphoreType.DMA((copies,)),
        ],
        name="front",
        **params(4 * elements * trace * quad, 4 * elements * trace, FRONT_VMEM),
    )(*(pltpu.with_memory_space_constraint(x, pltpu.HBM) for x in fetched))


def apply(field, below, above, connect, stiff, perm, stiff_ref):
    elements = connect.shape[1]
    cut = FIELDS * HIS
    small = shape(cut, LANES)
    return pl.pallas_call(
        functools.partial(apply_kernel, chunk=512),
        out_shape=[small, small, small, shape(3, RIM), shape(3, RIM)],
        name="apply",
        **params(16 * elements * LANES * cut, 24 * elements),
    )(field, below, above, connect, stiff, perm, stiff_ref)


def exchanged(up, low):
    count = lax.axis_size("sub")
    below = lax.ppermute(up, "sub", [(i, (i + 1) % count) for i in range(count)])
    above = lax.ppermute(low, "sub", [(i, (i - 1) % count) for i in range(count)])
    return below, above


def per_device(
    adjoint_traces,
    primal_traces,
    jacobian,
    stiffness,
    connect,
    shared_perm,
    wall_owner,
    wall_patch,
    w_trace,
    w_state,
    w_node,
    w_block,
    w_adjoint,
    stiff_ref,
):
    walls = wall_owner.shape[0]
    devices = lax.axis_size("dom") * lax.axis_size("sub")
    width = w_block.shape[1]
    jac = jacobian.reshape(1, -1)
    stiff = stiffness.reshape(1, -1)
    owner = wall_owner.reshape(1, -1)
    patch = wall_patch.reshape(1, -1)
    perm = shared_perm.reshape(1, -1)
    field, up, low, blocks = front(
        walls, adjoint_traces, primal_traces, jac, stiff, connect,
        w_trace, w_state, w_node.T, w_block, perm, stiff_ref, owner, patch,
    )
    below, above = exchanged(up, low)

    pieces = pl.pallas_call(
        wall_kernel,
        out_shape=[shape(devices * KEPT, width)] * GROUP,
        name="walls",
        **params(4 * walls * width * devices * PATCH_DEV, 8 * walls * width),
    )(blocks, owner, patch)
    *pieces, below, above = lax.optimization_barrier((*pieces, below, above))
    doms = lax.axis_size("dom")
    pieces = [
        pieces[0],
        *(
            lax.ppermute(pieces[k], "dom", [(i, i ^ k) for i in range(doms)])
            for k in range(1, GROUP)
        ),
    ]

    small = shape(FIELDS * HIS, LANES)
    base, scale, applied, up, low = apply(
        field, below, above, connect, stiff, perm, stiff_ref
    )
    conn_spec = pl.BlockSpec((4, walls), lambda s: (0, 0))
    payload = shape(devices, 2, ROWS // 2 * LANES)
    payload = pl.pallas_call(
        sums_kernel,
        grid=(1,),
        in_specs=[
            *[whole(small.shape)] * 3, *[whole(below.shape)] * 2, conn_spec,
            whole(owner.shape), whole(patch.shape), whole(perm.shape),
            *[whole(pieces[0].shape)] * GROUP,
        ],
        out_specs=whole(payload.shape),
        out_shape=payload,
        name="sums",
        **params(3000 * walls * LANES, 8 * devices * PATCH_DEV * width),
    )(base, scale, applied, below, above, connect, owner, patch, perm, *pieces)

    payload, up, low = lax.optimization_barrier((payload, up, low))
    got = lax.all_to_all(payload, ("dom", "sub"), split_axis=0, concat_axis=0, tiled=True)
    below, above = exchanged(up, low)
    adjoint = pl.pallas_call(
        adjoint_kernel,
        out_shape=shape(FIELDS, HIS * LANES),
        name="adjoint",
        **params(10**7, 10**5),
    )(base, scale, applied, below, above, perm)
    grad = pl.pallas_call(
        owner_kernel,
        out_shape=shape(PATCH_DEV, width),
        name="owners",
        **params(10**6, 4 * devices * ROWS * width),
    )(got, w_adjoint)
    return (grad, adjoint)


def solution(mesh):
    both = ("dom", "sub")
    return jax.shard_map(
        per_device,
        mesh=mesh,
        in_specs=(
            P(None, both),
            P(None, both),
            P(both),
            P(both),
            P(None, both),
            P("dom", "sub", None),
            P(both, None),
            P(both),
            P(),
            P(),
            P(),
            P(),
            P(),
            P(),
        ),
        out_specs=(P(both, None), P(None, both)),
        check_vma=False,
    )
```

```python
import functools

import jax
import jax.numpy as jnp
from jax import lax
from jax.experimental import pallas as pl
from jax.experimental.pallas import tpu as pltpu
from jax.sharding import PartitionSpec as P

PATCH_DEV = 16
LANES = 128
HIS = 16
FIELDS = 3
RIM = 256
PIECES = 8
GROUP = 2
KEPT = PATCH_DEV // GROUP
FRONT_VMEM = 40
ROWS = KEPT + 2

mass_shift = 0.5
relax = 0.7

f32 = jnp.float32
bf16 = jnp.bfloat16

NN = (((1,), (0,)), ((), ()))
NT = (((1,), (1,)), ((), ()))


def mxu(a, b, dims):
    return lax.dot_general(a, b, dims, preferred_element_type=f32)


def exact(a, b, dims):
    return lax.dot_general(
        a, b, dims, preferred_element_type=f32, precision=lax.Precision.HIGHEST
    )


def halves(x):
    top = x.astype(bf16).astype(f32)
    return top, x - top


def one_hot(index_row, rows):
    shape = (rows, index_row.shape[1])
    wanted = jnp.broadcast_to(index_row.astype(jnp.int16), shape)
    hit = wanted == lax.broadcasted_iota(jnp.int16, shape, 0)
    return jnp.where(hit, jnp.ones(shape, bf16), jnp.zeros(shape, bf16))


def placed(index_row, value_rows):
    shape = (HIS, index_row.shape[1])
    wanted = jnp.broadcast_to(index_row.astype(jnp.int16), shape)
    hit = wanted == lax.broadcasted_iota(jnp.int16, shape, 0)
    zero = jnp.zeros(shape, bf16)
    return jnp.concatenate(
        [jnp.where(hit, jnp.broadcast_to(v, shape).astype(bf16), zero) for v in value_rows], axis=0
    )


def rim_rows(field, first):
    count = field.shape[0] // HIS
    parts = [
        jnp.concatenate([field[f * HIS + first + k : f * HIS + first + k + 1] for f in range(count)], 0)
        for k in range(2)
    ]
    return jnp.concatenate(parts, axis=1)


def reorder(rows, perm_row, dims):
    count = rows.shape[0]
    table = one_hot(perm_row, RIM)
    first, rest = halves(rows)
    second, third = halves(rest)
    pad = jnp.zeros((-count % 8, RIM), f32)
    stack = jnp.concatenate([first, pad, second, pad, third, pad], axis=0).astype(bf16)
    out = mxu(stack, table, dims)
    step = count + (-count % 8)
    return out[:count] + out[step : step + count] + out[2 * step : 2 * step + count]


def rims(below, above, perm_row):
    count = below.shape[0]
    place = lax.axis_index("sub")
    last = lax.axis_size("sub") - 1
    below = jnp.where(place == 0, 0.0, below)
    above = jnp.where(place == last, 0.0, above)
    low = reorder(below, perm_row, NT)
    parts = []
    for f in range(count):
        parts += [
            low[f : f + 1, :LANES],
            low[f : f + 1, LANES:],
            jnp.zeros((HIS - 4, LANES), f32),
            above[f : f + 1, :LANES],
            above[f : f + 1, LANES:],
        ]
    return jnp.concatenate(parts, axis=0)


def write_message(message, rims, perm, conn, owner, patch):
    message[:8] = jnp.concatenate([rims, perm[...].astype(f32), jnp.zeros((1, RIM), f32)], axis=0)
    for i in range(PIECES):
        cols = slice(i * RIM, (i + 1) * RIM)
        message[8 + 4 * i : 12 + 4 * i] = conn[:, cols].astype(f32)
        target = owner[:, cols] * PATCH_DEV + patch[:, cols]
        message[8 + 4 * PIECES + i : 9 + 4 * PIECES + i] = target.astype(f32)


def read_message(message):
    pairs = range(PIECES // 2)
    slots = jnp.concatenate([message[8 + 8 * j : 16 + 8 * j] for j in pairs], axis=1)
    first = 8 + 4 * PIECES
    targets = [
        jnp.concatenate([message[first + 2 * j + k : first + 2 * j + k + 1] for j in pairs], axis=1)
        for k in range(2)
    ]
    return slots.astype(jnp.int32), [x.astype(jnp.int32) for x in targets]


def front_kernel(*refs, walls):
    count = (len(refs) - 6) // 2
    sources, w_node, (field, up, low, wall_product) = refs[:count], refs[count], refs[count + 1 : count + 5]
    held, sems = refs[count + 5 : -1], refs[-1]
    traces, states, jac, stiff, conn, w_trace, w_state, perm, ref, owner, patch = held
    cuts = [0, walls // 4, *range(walls, traces.shape[1] + 1, walls)]
    spans = [slice(p, q) for p, q in zip(cuts, cuts[1:])]
    copies = []

    def fetch(k, span=None):
        source, target = sources[k], held[k]
        if span is not None:
            source, target = source.at[:, span], target.at[:, span]
        copy = pltpu.make_async_copy(source, target, sems.at[len(copies)])
        copy.start()
        copies.append(copy)
        return copy

    weights = [fetch(5)]
    first = [fetch(0, spans[0])]
    weights.append(fetch(6))
    first += [fetch(1, spans[0]), fetch(2)]
    small = [fetch(k) for k in (3, 4)]
    later = [[fetch(0, span), fetch(1, span)] for span in spans[1:]]
    last = [fetch(k) for k in (7, 8, 9, 10)]
    weights[0].wait()
    trace_t = w_trace[...].astype(f32).T.astype(bf16)
    weights[1].wait()
    state_t = w_state[...].astype(f32).T.astype(bf16)
    pad = jnp.zeros((4, w_node.shape[1]), f32)
    node_t = jnp.concatenate([w_node[...].astype(f32), pad], axis=0).astype(bf16)
    cut = FIELDS * HIS
    sums = [jnp.zeros((LANES, 2 * (cut + HIS)), f32) for _ in range(4)]
    for s, span in enumerate(spans):
        for copy in first if s == 0 else later[s - 1]:
            copy.wait()
        upsilon = mxu(trace_t, traces[:, span], NN)
        tangent = mxu(state_t, states[:, span], NN)
        product = (jac[:, span] * upsilon * tangent).astype(bf16)
        terms = mxu(node_t, product, NN)
        if s < 2:
            wall_product[:, span] = product
        if s == 0:
            for copy in small:
                copy.wait()
        top, rest = halves(terms)
        stiff_top, stiff_rest = halves(stiff[:, span])
        slots = conn[:, span]
        high, lane = slots >> 7, slots & (LANES - 1)
        for a in range(4):
            rows = [top[c * 4 + a : c * 4 + a + 1] for c in range(FIELDS)] + [stiff_top]
            rows += [rest[c * 4 + a : c * 4 + a + 1] for c in range(FIELDS)] + [stiff_rest]
            spread = placed(high[a : a + 1], rows)
            sums[a] += mxu(one_hot(lane[a : a + 1], LANES), spread, NT)

    for copy in last:
        copy.wait()
    sums = [x.T for x in sums]
    sums = [x[: cut + HIS] + x[cut + HIS :] for x in sums]
    sens = sums[0][:cut] + sums[1][:cut] + sums[2][:cut] + sums[3][:cut]
    diag = []
    for c in range(FIELDS):
        total = jnp.zeros((HIS, LANES), f32)
        for a in range(4):
            i = c * 4 + a
            total += ref[i : i + 1, i : i + 1] * sums[a][cut:]
        diag.append(total)
    both = jnp.concatenate([sens] + diag, axis=0)
    field[...] = both
    write_message(up, rim_rows(both, HIS - 2), perm, conn, owner, patch)
    write_message(low, reorder(rim_rows(both, 0), perm[...], NN), perm, conn, owner, patch)


def group_place():
    return lax.axis_index("dom") % GROUP


def wall_kernel(product, w_block, owner, patch, *sums):
    rows = sums[0].shape[0]
    owners = rows // KEPT
    slot = (patch[...] // KEPT ^ group_place()) * rows + patch[...] % KEPT * owners + owner[...]
    blocks = mxu(w_block[...].astype(f32).T.astype(bf16), product[...], NN)
    top, rest = halves(blocks)
    both = jnp.concatenate([top, rest], axis=0).astype(bf16)
    for k in range(GROUP):
        out = mxu(one_hot(slot - k * rows, rows), both, NT)
        sums[k][...] = out[:, :LANES] + out[:, LANES:]


def all_lines(table):
    return [[(h, table[f * HIS + h : f * HIS + h + 1]) for h in range(HIS)] for f in range(FIELDS)]


def rim_lines(rims, first):
    return [
        [(first + k, rims[f : f + 1, k * LANES : (k + 1) * LANES]) for k in range(2)]
        for f in range(FIELDS)
    ]


def looked_up(table, slots):
    n = slots.shape[1] // LANES
    rows = [[] for _ in table]
    for k in range(n):
        here = slots[:, k * LANES : (k + 1) * LANES]
        high, lane = here >> 7, here & (LANES - 1)
        for f, lines in enumerate(table):
            got = jnp.zeros((8, LANES), f32)
            for h, line in lines:
                line = jnp.broadcast_to(line, (8, LANES))
                picked = jnp.take_along_axis(line, lane, axis=1, mode="promise_in_bounds")
                got = jnp.where(high == h, picked, got)
            rows[f].append(got)
    return [jnp.concatenate(r, axis=1) for r in rows]


def apply_kernel(
    field, below, above, conn, stiff, perm, ref,
    base, scale, applied, up, low,
    *, chunk,
):
    shared = field[...] + rims(below[:6], above[:6], perm[...])
    cut = FIELDS * HIS
    sens, diag = shared[:cut], shared[cut:] + mass_shift
    over = relax / diag
    psi = over * sens
    base[...] = psi + over * (sens - mass_shift * psi)
    scale[...] = over

    index = lax.broadcasted_iota(jnp.int32, (24, 12), 0)
    pick = (index // 8 * 4 + index % 4) == lax.broadcasted_iota(jnp.int32, (24, 12), 1)
    pick = pick.astype(f32)
    wide = exact(exact(pick, ref[...], NN), pick, NT)
    half_of_row = lax.broadcasted_iota(jnp.int32, (24, 24), 0) // 4 % 2
    half_of_col = lax.broadcasted_iota(jnp.int32, (24, 24), 1) // 4 % 2
    wide = jnp.where(half_of_row == half_of_col, wide, 0.0)
    wide_top, wide_rest = halves(wide)
    wide = jnp.concatenate(
        [
            jnp.concatenate([wide_top, wide_top], axis=1),
            jnp.concatenate([wide_rest, wide_rest], axis=1),
        ],
        axis=0,
    ).astype(bf16)

    half = conn.shape[1] // 2
    total = jnp.zeros((cut, LANES), f32)

    def prepare(start):
        first = slice(start, start + chunk)
        second = slice(half + start, half + start + chunk)
        slots = jnp.concatenate([conn[:, first], conn[:, second]], axis=0)
        values = jnp.concatenate(looked_up(all_lines(psi), slots), axis=0)
        top, rest = halves(values)
        pushed = mxu(wide, jnp.concatenate([top, rest], axis=0).astype(bf16), NN)
        pushed = pushed[:24] + pushed[24:]
        in_first = lax.broadcasted_iota(jnp.int32, (8, chunk), 0) < 4
        weight = jnp.where(in_first, stiff[:, first], stiff[:, second])
        pushed = pushed * jnp.concatenate([weight] * FIELDS, axis=0)
        return slots, halves(pushed)

    ready = prepare(0)
    for start in range(0, half, chunk):
        slots, parts = ready
        if start + chunk < half:
            ready = prepare(start + chunk)
        high, lane = slots >> 7, slots & (LANES - 1)
        for row in range(8):
            rows = [x[c * 8 + row : c * 8 + row + 1] for x in parts for c in range(FIELDS)]
            spread = placed(high[row : row + 1], rows)
            out = mxu(spread, one_hot(lane[row : row + 1], LANES), NT)
            total += out[:cut] + out[cut:]
    applied[...] = total
    up[...] = rim_rows(total, HIS - 2)
    low[...] = reorder(rim_rows(total, 0), perm[...], NN)


def patch_parts(values, targets, owners):
    parts = [halves(v) for v in values]
    out = []
    for k, target in enumerate(targets):
        rows = [
            parts[c][p][4 * k + a : 4 * k + a + 1]
            for p in range(2)
            for c in range(FIELDS)
            for a in range(4)
        ]
        out.append((one_hot(target // PATCH_DEV, owners), placed(target % PATCH_DEV, rows)))
    return out


def sums_kernel(base, scale, applied, below, above, conn, owner, patch, perm, *rest):
    *pieces, payload = rest
    owners = payload.shape[0]
    change = scale[...] * applied[...]
    psi = base[...] - change
    walls = owner.shape[1]
    half = walls // 2
    slots = jnp.concatenate([conn[:, :half], conn[:, half:walls]], axis=0)
    target = owner[...] * PATCH_DEV + patch[...]
    values = looked_up(all_lines(psi), slots)
    terms = patch_parts(values, [target[:, :half], target[:, half:]], owners)

    place = lax.axis_index("sub")
    last = lax.axis_size("sub") - 1
    lower = reorder(rim_rows(-change, 0), perm[...], NN)
    lower = jnp.where(place == 0, 0.0, lower)
    slots, targets = read_message(below)
    terms += patch_parts(looked_up(rim_lines(lower, HIS - 2), slots), targets, owners)
    upper = reorder(rim_rows(-change, HIS - 2), above[6:7].astype(jnp.int32), NT)
    upper = jnp.where(place == last, 0.0, upper)
    slots, targets = read_message(above)
    terms += patch_parts(looked_up(rim_lines(upper, 0), slots), targets, owners)
    left, right = (jnp.concatenate(x, axis=1) for x in zip(*terms))
    total = mxu(left, right, NT)
    total = total[:, : 12 * PATCH_DEV] + total[:, 12 * PATCH_DEV :]

    total = jnp.concatenate([total, jnp.zeros((owners, 4 * PATCH_DEV), f32)], axis=1)
    kept = pieces[0][...]
    for piece in pieces[1:]:
        kept += piece[...]
    for k in range(2):
        rows = [kept[r * owners : (r + 1) * owners] for r in range(k, KEPT, 2)]
        rows.append(total[:, k * LANES : (k + 1) * LANES])
        payload[:, k : k + 1, :] = jnp.concatenate(rows, axis=1).reshape(owners, 1, ROWS // 2 * LANES)


def adjoint_kernel(base, scale, applied, below, above, perm, adjoint):
    psi = base[...] - scale[...] * (applied[...] + rims(below[...], above[...], perm[...]))
    for c in range(FIELDS):
        for h in range(HIS):
            adjoint[c : c + 1, h * LANES : (h + 1) * LANES] = psi[c * HIS + h : c * HIS + h + 1]


def owner_kernel(got, w_adjoint, out):
    doms = lax.axis_size("dom")
    subs = got.shape[0] // doms
    by_dom = []
    for d in range(doms):
        total = got[d * subs]
        for s in range(1, subs):
            total += got[d * subs + s]
        by_dom.append(total)
    parts = []
    for g in range(GROUP):
        total = by_dom[g]
        for d in range(g + GROUP, doms, GROUP):
            total += by_dom[d]
        parts += [total[r % 2 : r % 2 + 1, r // 2 * LANES : (r // 2 + 1) * LANES] for r in range(KEPT)]
    everything = by_dom[0]
    for d in range(1, doms):
        everything += by_dom[d]
    everything = everything[:, KEPT // 2 * LANES :]
    shape = (PATCH_DEV, LANES)
    mine = lax.broadcasted_iota(jnp.int32, shape, 1) % PATCH_DEV == lax.broadcasted_iota(
        jnp.int32, shape, 0
    )
    spread = [
        jnp.where(mine, everything[k : k + 1], 0.0) for k in range(2)
    ]
    shape = (2 * LANES, w_adjoint.shape[0])
    rows = lax.broadcasted_iota(jnp.int32, shape, 0) // PATCH_DEV
    pick = (rows == lax.broadcasted_iota(jnp.int32, shape, 1)).astype(f32)
    weights = exact(pick, w_adjoint[...].astype(f32), NN)
    out[...] = jnp.concatenate(parts, axis=0) + exact(
        jnp.concatenate(spread, axis=1), weights, NN
    )


def params(flops, bytes_accessed, vmem=24):
    return dict(
        compiler_params=pltpu.CompilerParams(vmem_limit_bytes=vmem * 2**20),
        cost_estimate=pl.CostEstimate(
            flops=flops, bytes_accessed=bytes_accessed, transcendentals=0
        ),
    )


def shape(*dims):
    return jax.ShapeDtypeStruct(dims, f32)


def front(walls, node_t, *fetched):
    trace, elements = fetched[0].shape
    quad = fetched[5].shape[1]
    message = shape(8 + 5 * PIECES, RIM)
    product = jax.ShapeDtypeStruct((quad, walls), bf16)
    outs = [shape(2 * FIELDS * HIS, LANES), message, message, product]
    copies = len(fetched) + 2 * (elements // walls)
    return pl.pallas_call(
        functools.partial(front_kernel, walls=walls),
        in_specs=[pl.BlockSpec(memory_space=pl.ANY)] * len(fetched)
        + [pl.BlockSpec(memory_space=pltpu.VMEM)],
        out_shape=outs,
        scratch_shapes=[
            *(pltpu.VMEM(x.shape, x.dtype) for x in fetched),
            pltpu.SemaphoreType.DMA((copies,)),
        ],
        name="front",
        **params(4 * elements * trace * quad, 4 * elements * trace, FRONT_VMEM),
    )(*(pltpu.with_memory_space_constraint(x, pltpu.HBM) for x in fetched), node_t)


def apply(field, below, above, connect, stiff, perm, stiff_ref):
    elements = connect.shape[1]
    cut = FIELDS * HIS
    small = shape(cut, LANES)
    return pl.pallas_call(
        functools.partial(apply_kernel, chunk=512),
        out_shape=[small, small, small, shape(3, RIM), shape(3, RIM)],
        name="apply",
        **params(16 * elements * LANES * cut, 24 * elements),
    )(field, below, above, connect, stiff, perm, stiff_ref)


def exchanged(up, low):
    count = lax.axis_size("sub")
    below = lax.ppermute(up, "sub", [(i, (i + 1) % count) for i in range(count)])
    above = lax.ppermute(low, "sub", [(i, (i - 1) % count) for i in range(count)])
    return below, above


def per_device(
    adjoint_traces,
    primal_traces,
    jacobian,
    stiffness,
    connect,
    shared_perm,
    wall_owner,
    wall_patch,
    w_trace,
    w_state,
    w_node,
    w_block,
    w_adjoint,
    stiff_ref,
):
    walls = wall_owner.shape[0]
    devices = lax.axis_size("dom") * lax.axis_size("sub")
    width = w_block.shape[1]
    jac = jacobian.reshape(1, -1)
    stiff = stiffness.reshape(1, -1)
    owner = wall_owner.reshape(1, -1)
    patch = wall_patch.reshape(1, -1)
    perm = shared_perm.reshape(1, -1)
    field, up, low, product = front(
        walls, w_node.T, adjoint_traces, primal_traces, jac, stiff, connect,
        w_trace, w_state, perm, stiff_ref, owner, patch,
    )
    below, above = exchanged(up, low)

    pieces = pl.pallas_call(
        wall_kernel,
        out_shape=[shape(devices * KEPT, width)] * GROUP,
        name="walls",
        **params(4 * walls * width * devices * PATCH_DEV, 8 * walls * width),
    )(product, w_block, owner, patch)
    *pieces, below, above = lax.optimization_barrier((*pieces, below, above))
    doms = lax.axis_size("dom")
    pieces = [
        pieces[0],
        *(
            lax.ppermute(pieces[k], "dom", [(i, i ^ k) for i in range(doms)])
            for k in range(1, GROUP)
        ),
    ]

    small = shape(FIELDS * HIS, LANES)
    base, scale, applied, up, low = apply(
        field, below, above, connect, stiff, perm, stiff_ref
    )
    payload = shape(devices, 2, ROWS // 2 * LANES)
    payload = pl.pallas_call(
        sums_kernel,
        out_shape=payload,
        name="sums",
        **params(3000 * walls * LANES, 8 * devices * PATCH_DEV * width),
    )(base, scale, applied, below, above, connect, owner, patch, perm, *pieces)

    payload, up, low = lax.optimization_barrier((payload, up, low))
    got = lax.all_to_all(payload, ("dom", "sub"), split_axis=0, concat_axis=0, tiled=True)
    below, above = exchanged(up, low)
    adjoint = pl.pallas_call(
        adjoint_kernel,
        out_shape=shape(FIELDS, HIS * LANES),
        name="adjoint",
        **params(10**7, 10**5),
    )(base, scale, applied, below, above, perm)
    grad = pl.pallas_call(
        owner_kernel,
        out_shape=shape(PATCH_DEV, width),
        name="owners",
        **params(10**6, 4 * devices * ROWS * width),
    )(got, w_adjoint)
    return (grad, adjoint)


def solution(mesh):
    both = ("dom", "sub")
    return jax.shard_map(
        per_device,
        mesh=mesh,
        in_specs=(
            P(None, both),
            P(None, both),
            P(both),
            P(both),
            P(None, both),
            P("dom", "sub", None),
            P(both, None),
            P(both),
            P(),
            P(),
            P(),
            P(),
            P(),
            P(),
        ),
        out_specs=(P(both, None), P(None, both)),
        check_vma=False,
    )
```
